32 devices in a mesh: ctx: 8 (over z, core), wt: 4 (over y, x).
Axes of the slice: x: 2, y: 2, z: 4, core: 2. Of those that a mesh axis runs over, the one named last changes fastest.
Arguments:
- tokens: bfloat16 [4, 2048, 1536], P('wt', 'ctx'), may hold values from -6 to 6
- segments: int32 [4, 2048], P('wt'), may hold values from 0 to 2, as said below
- routes: int32 [4, 2048, 2], P('wt', 'ctx'), may hold values from 0 to 3, all different within a row; in each aligned block of 256 rows (0 to 255, 256 to 511, ..., all dimensions but the last counted through in order) at most 160 rows name the same one
- route_weights: float32 [4, 2048, 2], P('wt', 'ctx'), may hold values from 0.3 to 1
- gain_attn: bfloat16 [1536], P('wt'), may hold values from 0.25 to 1.75
- w_query: bfloat16 [1536, 1536], P('wt'), may hold values from -0.15625 to 0.15625
- w_key: bfloat16 [1536, 512], P('wt'), may hold values from -0.15625 to 0.15625
- w_value: bfloat16 [1536, 512], P('wt'), may hold values from -0.15625 to 0.15625
- w_out: bfloat16 [1536, 1536], P('wt'), may hold values from -0.625 to 0.625
- gain_ffn: bfloat16 [1536], P('wt'), may hold values from 0.25 to 1.75
- w_gate: bfloat16 [4, 1536, 1024], P(None, None, 'wt'), may hold values from -0.15625 to 0.15625
- w_up: bfloat16 [4, 1536, 1024], P(None, None, 'wt'), may hold values from -0.15625 to 0.15625
- w_down: bfloat16 [4, 1024, 1536], P(None, 'wt'), may hold values from -0.1875 to 0.1875
- cotangent: bfloat16 [4, 2048, 1536], P('wt', 'ctx'), may hold values from -6 to 6
Outputs:
- output: bfloat16 [4, 2048, 1536], P('wt', 'ctx')
- grad_tokens: float32 [4, 2048, 1536], P('wt', 'ctx')
- grad_gain_attn: float32 [1536], P('wt')
- grad_w_query: float32 [1536, 1536], P('wt')
- grad_w_key: float32 [1536, 512], P('wt')
- grad_w_value: float32 [1536, 512], P('wt')
- grad_w_out: float32 [1536, 1536], P('wt')
- grad_gain_ffn: float32 [1536], P('wt')
- grad_w_gate: float32 [4, 1536, 1024], P(None, None, 'wt')
- grad_w_up: float32 [4, 1536, 1024], P(None, None, 'wt')
- grad_w_down: float32 [4, 1024, 1536], P(None, 'wt')
The draws below stay inside these ranges and needn't reach their ends.
Inputs may be any that keep to these rules, and one draw needn't show every extreme that they name: `segments`: numbers in position order (not in the dealt order of the token arrays); they never fall along a sequence and rise by at most one from a position to the next, start at 0, and the first document covers positions 0 to 1151. Every sequence's last position holds (896) // 400. `routes`: the two experts of a row differ; among the rows of one device no expert is named more than 160 times, a bound that some block reaches.
All inputs are finite; a program needn't handle non-finite values.
Results may differ from the reference program's by a relative error of at most 0.014.
Values may be sent and summed in bfloat16 or wider, within the bound.
No kernel may reach another device: no remote copies, remote signals or barrier semaphores. Data moves between devices by JAX's collectives and lax.ppermute only.
A program may use at most 320 MiB of HBM per device.

```python
import math
import jax
import jax.numpy as jnp
import numpy as np
from jax import lax

D = 1536
HEADS = 24
KV_HEADS = 8
HEAD_DIM = 64
FF = 1024
EXPERTS = 4
DOC_MEAN = 400
TOK_DEV = 256
LEN = 2048
SEQS = 4
CAP = 160
N_CTX = 8


def draw_segments(key, part):
    key = jax.random.fold_in(key, 11)
    first_len = LEN // 2 + TOK_DEV // 2
    doc_count = (LEN - first_len) // DOC_MEAN
    spare = LEN - first_len - 1
    seq_keys = jax.random.split(key, SEQS)
    orders = jax.vmap(lambda one: jax.random.permutation(one, spare))(seq_keys)
    later_cuts = (orders < doc_count - 1).astype(jnp.int32)
    before = jnp.zeros((SEQS, first_len), jnp.int32)
    forced = jnp.ones((SEQS, 1), jnp.int32)
    cuts = jnp.concatenate([before, forced, later_cuts], axis=1)
    return jnp.cumsum(cuts, axis=1).astype(jnp.int32)


def level_of(own_key, shape, pieces, smallest, largest):
    level, own = 1.0, jax.random.fold_in(own_key, 6)
    for position, shards_of in pieces:
        heights = jnp.exp(jax.random.uniform(jax.random.fold_in(own, position), (shards_of,), jnp.float32, smallest / len(pieces), largest / len(pieces)))
        level = level * jnp.repeat(heights, shape[position] // shards_of).reshape([-1 if axis == position else 1 for axis in range(len(shape))])
    return level


def assign_block(stream_key, own, number, rows, amount, top, most, lean):
    order = jax.random.permutation(stream_key, amount)
    crowded, common = shares(amount, rows * top, most, lean, True), shares(amount, rows * top, most, lean, False)
    places = jnp.arange(amount)

    def named(lengths, rotation):
        used = int((lengths > 0).sum())
        fixed = max(1, used // 4)
        moved = fixed + (places - fixed + rotation * (used - fixed)) % max(1, amount - fixed)
        return jnp.zeros((amount,), jnp.int32).at[order[jnp.where(places < fixed, places, moved)]].set(jnp.asarray(lengths, jnp.int32))

    lengths = jnp.where(number % 4 == 0, named(crowded, number // 4), named(common, number - number // 4 - 1))
    mixed = jax.random.permutation(jax.random.fold_in(own, 3), amount)
    source_of, sink = mixed[0:amount // 2 * 2:2], mixed[1:amount // 2 * 2:2]
    margin = jnp.minimum(lengths[source_of] - 1, most - lengths[sink]) // 2
    margin = jnp.where((source_of == order[0]) | (sink == order[0]) | (lengths[sink] == 0), 0, jnp.maximum(margin, 0))
    moved = jax.random.randint(jax.random.fold_in(own, 4), (amount // 2,), 0, 1 << 20) % (margin + 1)
    lengths = lengths.at[source_of].add(-moved).at[sink].add(moved)
    labels = jnp.searchsorted(jnp.cumsum(lengths), jnp.arange(rows * top), side="right").astype(jnp.int32)
    table = labels.reshape(top, rows).T
    table = table[jax.random.permutation(jax.random.fold_in(own, 1), rows)]
    rotation = jax.random.randint(jax.random.fold_in(own, 2), (rows, 1), 0, top)
    return jnp.take_along_axis(table, (jnp.arange(top)[None, :] + rotation) % top, axis=1)


def shares(count, total, bound, lean, full):
    weights = [(1 << 20) // math.isqrt(standing ** lean) + 1 for standing in range(1, count + 1)]
    largest = bound if full else min(bound, max(-(-total // count), total * weights[0] // sum(weights)))
    least = 1 if total - largest >= count - 1 else 0
    counts, surplus = [largest] + [least] * (count - 1), total - largest - least * (count - 1)
    while surplus > 0:
        candidates = [i for i in range(1, count) if counts[i] < largest] or [i for i in range(1, count) if counts[i] < bound]
        whole, remaining = sum([weights[i] for i in candidates]), surplus
        for i in candidates:
            extra = min(bound - counts[i], max(1, remaining * weights[i] // whole), surplus)
            counts[i] = counts[i] + extra
            surplus = surplus - extra
    return np.array(counts)


def normal_values(rng, shape, scale, reach, cuts=(), held_as=jnp.bfloat16):
    entries = scale * jax.random.normal(rng, shape, jnp.float32)
    if cuts:
        entries = entries * level_of(rng, shape, cuts, -0.22, 0.18)
    return jnp.clip(entries, -reach, reach).astype(held_as)


def setup_inputs(seed: int = 0) -> dict:
    splits = jax.random.split(jax.random.key(seed), 15)
    tokens = normal_values(splits[0], (SEQS, LEN, D), 1.0, 6.0, ((0, 4), (1, 8)))
    segments = draw_segments(jax.random.fold_in(splits[14], 71), 0)
    routes_keys = jax.random.split(jax.random.fold_in(splits[2], 1), SEQS * LEN // TOK_DEV)
    routes_turns = jax.random.permutation(jax.random.fold_in(splits[2], 3), SEQS * LEN // TOK_DEV)
    routes = jax.vmap(lambda own, number: assign_block(jax.random.fold_in(splits[2], 2), own, number, TOK_DEV, EXPERTS, 2, CAP, 1))(routes_keys, routes_turns).reshape((SEQS, LEN, 2))
    route_weights = jnp.clip(jnp.exp(math.log(1.0) - 1.2039728 * jax.random.uniform(splits[3], (SEQS, LEN, 2), jnp.float32) ** level_of(splits[3], (SEQS, LEN, 2), ((0, 4), (1, 8)), -0.2, 0.2)), 0.3, 1.0)
    gain_attn = jnp.clip(1.0 + 0.15 * jax.random.normal(splits[4], (D,), jnp.float32), 0.25, 1.75).astype(jnp.bfloat16)
    w_query = normal_values(splits[5], (D, D), D ** -0.5, 0.15625, ((0, 4),))
    w_key = normal_values(splits[6], (D, KV_HEADS * HEAD_DIM), D ** -0.5, 0.15625, ((0, 4),))
    w_value = normal_values(splits[7], (D, KV_HEADS * HEAD_DIM), D ** -0.5, 0.15625, ((0, 4),))
    w_out = normal_values(splits[8], (D, D), (D // 16) ** -0.5, 0.625, ((0, 4),))
    gain_ffn = jnp.clip(1.0 + 0.15 * jax.random.normal(splits[9], (D,), jnp.float32), 0.25, 1.75).astype(jnp.bfloat16)
    w_gate = normal_values(splits[10], (EXPERTS, D, FF), D ** -0.5, 0.15625, ((2, 4),))
    w_up = normal_values(splits[11], (EXPERTS, D, FF), D ** -0.5, 0.15625, ((2, 4),))
    w_down = normal_values(splits[12], (EXPERTS, FF, D), FF ** -0.5, 0.1875, ((1, 4),))
    cotangent = normal_values(splits[13], (SEQS, LEN, D), 1.0, 6.0, ((0, 4), (1, 8)))
    return dict(tokens=tokens, segments=segments, routes=routes, route_weights=route_weights, gain_attn=gain_attn, w_query=w_query, w_key=w_key, w_value=w_value, w_out=w_out, gain_ffn=gain_ffn, w_gate=w_gate, w_up=w_up, w_down=w_down, cotangent=cotangent)


EPSILON = 1e-06
PRECISE = lax.Precision.HIGHEST
NEG_LARGE = -1e+30

@jax.custom_vjp
def low(v):
    return lax.optimization_barrier(v.astype(jnp.bfloat16)).astype(jnp.float32)

@jax.custom_vjp
def low_back(v):
    return v

def low_keep(v):
    return (low(v), None)

def low_pass(kept, grad):
    return (grad,)

def back_keep(v):
    return (v, None)

def back_low(kept, grad):
    return (low(grad),)
low.defvjp(low_keep, low_pass)
low_back.defvjp(back_keep, back_low)

def positions(count, shard, ctx_count, offset):
    index = jnp.arange(count, dtype=jnp.int32) + offset
    device = index // shard
    inner = index % shard
    half_len = shard // 2
    placed = jnp.where(inner < half_len, device * half_len + inner, (2 * ctx_count - 1 - device) * half_len + inner - half_len)
    return placed.astype(jnp.int32)

def inv_root(values):
    return lax.rsqrt(lax.optimization_barrier(jnp.mean(values * values, axis=-1, keepdims=True)) + EPSILON)

def matmul(left, right):
    return jnp.dot(left, right, precision=PRECISE)

def sequence_layer(params, inputs):
    tokens_in, seg_row, route_ids, route_wts = inputs
    gain_a, weight_q, weight_k, weight_v, weight_o, gain_f, weight_g, weight_u, weight_d = params
    seq_len = tokens_in.shape[0]
    group = HEADS // KV_HEADS
    scale = HEAD_DIM ** (-0.5)
    normed = low(tokens_in * inv_root(tokens_in) * gain_a)
    queries = low(low_back(matmul(normed, weight_q)))
    keys = low(low_back(matmul(normed, weight_k)))
    values = low(low_back(matmul(normed, weight_v)))
    where_pos = positions(seq_len, TOK_DEV, N_CTX, 0)
    where_seg = jnp.take(seg_row, where_pos)
    query_block = min(512, seq_len)
    block_count = seq_len // query_block
    key_heads = keys.reshape(seq_len, KV_HEADS, HEAD_DIM)
    value_heads = values.reshape(seq_len, KV_HEADS, HEAD_DIM)
    query_blocks = queries.reshape(block_count, query_block, KV_HEADS, group, HEAD_DIM)

    def attend(blocked):
        query_blk, query_pos, query_seg = blocked
        scores = scale * jnp.einsum('rgcd,kgd->gcrk', query_blk, key_heads, precision=PRECISE)
        scores = low_back(scores)
        allowed = (where_seg[None, :] == query_seg[:, None]) & (where_pos[None, :] <= query_pos[:, None])
        scores = jnp.where(allowed, scores, NEG_LARGE)
        probs = low(jax.nn.softmax(scores, axis=-1))
        mixed = jnp.einsum('gcrk,kgd->rgcd', probs, value_heads, precision=PRECISE)
        return mixed.reshape(query_block, HEADS * HEAD_DIM)
    attended = lax.map(jax.checkpoint(attend), (query_blocks, where_pos.reshape(block_count, query_block), where_seg.reshape(block_count, query_block)))
    attended = low(low_back(attended.reshape(seq_len, D)))
    resid = tokens_in + low_back(matmul(attended, weight_o))
    normed_f = low(resid * inv_root(resid) * gain_f)
    chosen = (route_ids[:, :, None] == jnp.arange(EXPERTS, dtype=jnp.int32)[None, None, :]).astype(jnp.float32)
    coeff = lax.optimization_barrier(jnp.sum(route_wts[:, :, None] * chosen, axis=1))
    gate_pre = low_back(jnp.einsum('rd,edf->erf', normed_f, weight_g, precision=PRECISE))
    up_pre = low_back(jnp.einsum('rd,edf->erf', normed_f, weight_u, precision=PRECISE))
    hidden = low(jax.nn.silu(gate_pre) * up_pre)
    expert_out = low_back(jnp.einsum('erf,efd->erd', hidden, weight_d, precision=PRECISE))
    mixture = jnp.einsum('re,erd->rd', coeff, expert_out, precision=PRECISE)
    return resid + mixture

def reference(tokens, segments, routes, route_weights, gain_attn, w_query, w_key, w_value, w_out, gain_ffn, w_gate, w_up, w_down, cotangent):
    params = tuple((array.astype(jnp.float32) for array in (gain_attn, w_query, w_key, w_value, w_out, gain_ffn, w_gate, w_up, w_down)))
    tokens_f = tokens.astype(jnp.float32)
    weights_f = route_weights.astype(jnp.float32)

    def forward(tokens_arg, *weights):
        return lax.map(lambda inputs: sequence_layer(weights, inputs), (tokens_arg, segments, routes, weights_f))
    result, pullback = jax.vjp(forward, tokens_f, *params)
    grads = pullback(cotangent.astype(jnp.float32))
    return (result.astype(jnp.bfloat16), grads[0], grads[1], grads[2], grads[3], grads[4], grads[5], grads[6], grads[7], grads[8], grads[9])
```

```python
import functools

import jax
import jax.numpy as jnp
from jax import lax
from jax.experimental import pallas as pl
from jax.experimental.pallas import tpu as pltpu
from jax.sharding import Mesh, PartitionSpec as P

HEADS = 24
KV_HEADS = 8
HEAD_DIM = 64
SCALE = HEAD_DIM ** -0.5
PAIRS = KV_HEADS // 2
EPSILON = 1e-06
NEG_LARGE = -1e30
VMEM_BYTES = 56 * 1024 * 1024
BF = jnp.bfloat16
F32 = jnp.float32

VMEM = pl.BlockSpec(memory_space=pltpu.VMEM)
SMEM = pl.BlockSpec(memory_space=pltpu.SMEM)
ANY = pl.BlockSpec(memory_space=pl.ANY)


def params():
    return pltpu.CompilerParams(vmem_limit_bytes=VMEM_BYTES)


def cost(flops, nbytes, trans=0):
    return pl.CostEstimate(flops=int(flops), bytes_accessed=int(nbytes), transcendentals=int(trans))


def shape(dims, dtype):
    return jax.ShapeDtypeStruct(tuple(dims), dtype)


def nn(a, b):
    return lax.dot_general(a, b, (((1,), (0,)), ((), ())), preferred_element_type=F32)


def nt(a, b):
    return lax.dot_general(a, b, (((1,), (1,)), ((), ())), preferred_element_type=F32)


def tn(a, b):
    return lax.dot_general(a, b, (((0,), (0,)), ((), ())), preferred_element_type=F32)


def inv_root(values):
    return lax.rsqrt(jnp.mean(values * values, axis=-1, keepdims=True) + EPSILON)


def swap(v, axis):
    return lax.ppermute(v, axis, [(0, 1), (1, 0)])


def to_y(v, d):
    n = lax.axis_size("y")
    return lax.ppermute(v, "y", [(i, (i + d) % n) for i in range(n)])


def from_y(v, d):
    n = lax.axis_size("y")
    return lax.ppermute(v, "y", [((i + d) % n, i) for i in range(n)])


def to_plane(v, dy, dx):
    n = lax.axis_size("y")
    if dy == 0:
        return swap(v, "x")
    if dx == 0:
        return to_y(v, dy)
    perm = [(2 * i + k, 2 * ((i + dy) % n) + (k ^ dx)) for i in range(n) for k in range(2)]
    return lax.ppermute(v, ("y", "x"), perm)


def z_move(v, d):
    n = lax.axis_size("z")
    return lax.ppermute(v, "z", [(i, i + d) for i in range(n) if 0 <= i + d < n])


def plane_gather(a, b):
    n = lax.axis_size("y")
    xa, xb = swap(a, "x"), swap(b, "x")
    got = {(0, 1): (xa, xb)}
    for d in range(1, n):
        ya, yb = from_y(a, d), from_y(b, d)
        got[(d, 0)] = (ya, yb)
        got[(d, 1)] = (from_y(xa, d), swap(yb, "x"))
    return got


def add_low(*terms):
    total = terms[0].astype(F32)
    for term in terms[1:]:
        total = total + term.astype(F32)
    return total.astype(terms[0].dtype)


def z_sum(v, z):
    n = lax.axis_size("z")
    if n == 4:
        inner = add_low(v, lax.ppermute(v, "z", [(0, 1), (3, 2)]))
        whole = add_low(inner, lax.ppermute(inner, "z", [(1, 2), (2, 1)]))
        outer = lax.ppermute(whole, "z", [(1, 0), (2, 3)])
        return jnp.where((z == 0) | (z == 3), outer, whole)
    bit = 1
    while bit < n:
        v = add_low(v, lax.ppermute(v, "z", [(i, i ^ bit) for i in range(n)]))
        bit *= 2
    return v


def plane_reduce(mine, other, y, x):
    n = lax.axis_size("y")
    rows = mine.shape[0] // (2 * n)
    h = rows // 2
    got = swap(other, "core")

    def block(dy, dx, part):
        place = (lax.rem(y + dy, n) * 2 + (x if dx == 0 else 1 - x)) * rows + part * h
        one = lax.dynamic_slice_in_dim(mine, place, h, 0)
        two = lax.dynamic_slice_in_dim(got, place, h, 0)
        return one.astype(F32) + two.astype(F32)

    sent_a = swap(jnp.stack([block(dy, 1, 0) for dy in range(n)]).astype(BF), "x")
    sent_b = [
        to_y(jnp.stack([block(d, 0, 1), block(d, 1, 1)]).astype(BF), d) for d in range(1, n)
    ]
    part_a = [block(dy, 0, 0) + sent_a[dy].astype(F32) for dy in range(n)]
    part_b = [
        block(0, dx, 1) + sum(got_b[dx].astype(F32) for got_b in sent_b) for dx in range(2)
    ]
    total_a = part_a[0]
    for d in range(1, n):
        total_a = total_a + to_y(part_a[d].astype(BF), d).astype(F32)
    total_b = part_b[0] + swap(part_b[1].astype(BF), "x").astype(F32)
    return total_a.astype(BF), total_b.astype(BF)


def whole_grad(mine, other, y, x, z, core):
    parts = []
    for part in plane_reduce(mine, other, y, x):
        part = z_sum(part, z)
        beside = swap(part, "core")
        parts.append((part, beside))
    a, b = parts
    own = jnp.concatenate([a[0], b[0]], axis=0).astype(F32)
    beside = jnp.concatenate([a[1], b[1]], axis=0).astype(F32)
    return jnp.where(
        core == 0,
        jnp.concatenate([own, beside], axis=1),
        jnp.concatenate([beside, own], axis=1),
    )


class Gathered:
    def __init__(self, own, halves, core_axis_halves):
        self.pieces = own + halves + core_axis_halves
        self.arrays = [piece[0] for piece in self.pieces]
        self.places = [piece[1:] for piece in self.pieces]


def gather_weight(own_full, own_a, own_b, half_width):
    rows = own_a.shape[0]
    own = [(array, (0, 0), 0, first) for array, first in own_full]
    mine, beside = [], []
    for where, (a, b) in plane_gather(own_a, own_b).items():
        for array, row in ((a, 0), (b, rows)):
            mine.append((array, where, row, "mine"))
            beside.append((swap(array, "core"), where, row, "other"))
    return Gathered(own, mine, beside)


def start_load(refs, places, dst, sems, ids, ny, shard, half_width):
    core, y, x = ids[1], ids[2], ids[3]
    copies = []
    for k, (ref, ((dy, dx), row, column)) in enumerate(zip(refs, places)):
        owner = lax.rem(y + dy, ny) * 2 + (x if dx == 0 else 1 - x)
        if column == "mine":
            column = core * half_width
        elif column == "other":
            column = (1 - core) * half_width
        if not isinstance(column, int):
            column = pl.multiple_of(column, 128)
        first = pl.multiple_of(owner * shard + row, 16)
        copy = pltpu.make_async_copy(
            ref,
            dst.at[pl.ds(first, ref.shape[0]), pl.ds(column, ref.shape[1])],
            sems.at[k],
        )
        copy.start()
        copies.append(copy)
    return copies


def gathered_matmul(lhs, weight, ids, ny, shard, width):
    count = len(weight.arrays)
    depth = 2 * ny * shard

    def kernel(ids_ref, lhs_ref, *refs):
        pieces, out_ref, held, sems = refs[:count], refs[count], refs[count + 1], refs[count + 2]
        for copy in start_load(pieces, weight.places, held, sems, ids_ref, ny, shard, width // 2):
            copy.wait()
        out_ref[...] = nn(lhs_ref[...], held[...]).astype(BF)

    return pl.pallas_call(
        kernel,
        out_shape=shape((lhs.shape[0], width), BF),
        in_specs=[SMEM, VMEM] + [ANY] * count,
        out_specs=VMEM,
        scratch_shapes=[pltpu.VMEM((depth, width), BF), pltpu.SemaphoreType.DMA((count,))],
        compiler_params=params(),
        cost_estimate=cost(2 * lhs.shape[0] * depth * width, 2 * depth * width + 2 * lhs.size),
        name="project",
    )(ids, lhs, *weight.arrays)


def load_keys(nz, half, ids, refs, kv, sems):
    z = ids[0]
    own, beside = refs[0], refs[1]
    slot = 2 * half

    def place(index, second):
        return kv.at[pl.ds(pl.multiple_of(index * slot + second * half, half), half)]

    always = []
    for k, ref in enumerate((own, beside)):
        always.append(pltpu.make_async_copy(ref.at[pl.ds(0, half)], place(0, k), sems.at[2 * k]))
        always.append(
            pltpu.make_async_copy(ref.at[pl.ds(half, half)], place(z + 1, k), sems.at[2 * k + 1])
        )
    for copy in always:
        copy.start()
    guarded = []
    for d in range(1, nz):
        group = refs[2 + 4 * (d - 1) : 2 + 4 * d]
        base = 4 + 4 * (d - 1)
        low = [pltpu.make_async_copy(group[k], place(d, k), sems.at[base + k]) for k in range(2)]
        high = [
            pltpu.make_async_copy(group[2 + k], place(z + 1 + d, k), sems.at[base + 2 + k])
            for k in range(2)
        ]
        guarded.append((d <= z, low))
        guarded.append((z + d < nz, high))
    for needed, copies in guarded:

        @pl.when(needed)
        def _():
            for copy in copies:
                copy.start()

    for copy in always:
        copy.wait()
    for needed, copies in guarded:

        @pl.when(needed)
        def _():
            for copy in copies:
                copy.wait()


def slot_range(nz, ids, tile):
    z, core = ids[0], ids[1]
    if tile == 0:
        return 0, z + 1
    last = (z == nz - 1) & (core == 1)
    return jnp.where(last, 0, z + 1), nz + 1


def fill_masks(nz, half, ids, seg_col, seg_row, masks):
    z, core = ids[0], ids[1]
    blocks = 4 * nz
    own = 2 * z + core
    for tile in range(2):
        query_block = own if tile == 0 else blocks - 1 - own
        query_at = pl.multiple_of(query_block * half, half)
        query_seg = seg_row[:, pl.ds(query_at, half)]
        query_pos = query_at + lax.broadcasted_iota(jnp.int32, (1, half), 1)
        first, end = slot_range(nz, ids, tile)

        def fill(index, unused):
            for second in range(2):
                side = core if second == 0 else 1 - core
                key_block = jnp.where(
                    index <= z, 2 * (z - index) + side, blocks - 1 - (2 * (index - 1) + side)
                )
                key_at = pl.multiple_of(key_block * half, half)
                key_seg = seg_col[pl.ds(key_at, half), :]
                key_pos = key_at + lax.broadcasted_iota(jnp.int32, (half, 1), 0)
                allowed = (key_seg == query_seg) & (key_pos <= query_pos)
                masks[tile, index, second * half : (second + 1) * half, :] = jnp.where(
                    allowed, 0.0, NEG_LARGE
                )
            return unused

        lax.fori_loop(first, end, fill, 0)


def split_heads(tile_rows, scale=None):
    half = tile_rows.shape[0]
    if scale is not None:
        tile_rows = tile_rows * jnp.asarray(scale, tile_rows.dtype)
    lane = lax.broadcasted_iota(jnp.int32, (half, 128), 1)
    zero = jnp.zeros((half, 128), tile_rows.dtype)
    t0, t1, t2 = (tile_rows[:, 128 * k : 128 * k + 128] for k in range(3))

    def low(t):
        return jnp.where(lane < 64, t, zero)

    def high(t):
        return jnp.where(lane >= 64, t, zero)

    straight = jnp.concatenate([low(t0), low(t1), high(t1), high(t2)], axis=0)
    crossed = jnp.concatenate([high(t0), low(t2)], axis=0)
    return straight, crossed


def join_heads(straight_t, crossed_t, half):
    def head(t, k, upper):
        return t[64 * upper : 64 * upper + 64, half * k : half * k + half]

    tiles = (
        (head(straight_t, 0, 0), head(crossed_t, 0, 1)),
        (head(straight_t, 1, 0), head(straight_t, 2, 1)),
        (head(crossed_t, 1, 0), head(straight_t, 3, 1)),
    )
    return jnp.concatenate([jnp.concatenate(t, axis=0).T for t in tiles], axis=1)


def cross(v):
    return jnp.concatenate([v[:, 64:], v[:, :64]], axis=1)


def attention_forward(q, keys, seg_col, seg_row, ids, nz):
    rows = q.shape[0]
    half = rows // 2
    slots = nz + 1
    count = len(keys)
    slot = 2 * half
    lanes = 6 * half

    def kernel(ids_ref, q_ref, col_ref, row_ref, *refs):
        key_refs = refs[:count]
        out_ref, lse_ref, kv, scores, masks, sems = refs[count:]
        fill_masks(nz, half, ids_ref, col_ref, row_ref, masks)
        load_keys(nz, half, ids_ref, key_refs, kv, sems)
        for tile in range(2):
            first, end = slot_range(nz, ids_ref, tile)
            for pair in range(PAIRS):
                straight, crossed = split_heads(
                    q_ref[tile * half : (tile + 1) * half, 384 * pair : 384 * pair + 384], SCALE
                )

                def score(index, peak):
                    at = pl.ds(pl.multiple_of(index * slot, slot), slot)
                    k = kv[at, 128 * pair : 128 * pair + 128]
                    mask = masks[tile, index]
                    s = jnp.concatenate([nt(k, straight), nt(cross(k), crossed)], axis=1)
                    s = s + jnp.concatenate([mask] * 6, axis=1)
                    scores[index] = s
                    return jnp.maximum(peak, jnp.max(s, axis=0, keepdims=True))

                peak = lax.fori_loop(
                    first, end, score, jnp.full((1, lanes), NEG_LARGE, F32)
                )

                def mix(index, carry):
                    mass, out_s, out_c = carry
                    at = pl.ds(pl.multiple_of(index * slot, slot), slot)
                    v = kv[at, 512 + 128 * pair : 512 + 128 * pair + 128]
                    p = jnp.exp(scores[index] - peak)
                    mass = mass + jnp.sum(p, axis=0, keepdims=True)
                    p = p.astype(BF)
                    v_t = v.T
                    out_s = out_s + nn(v_t, p[:, : 4 * half])
                    out_c = out_c + nn(
                        jnp.concatenate([v_t[64:], v_t[:64]], axis=0), p[:, 4 * half :]
                    )
                    return mass, out_s, out_c

                mass, out_s, out_c = lax.fori_loop(
                    first,
                    end,
                    mix,
                    (
                        jnp.zeros((1, lanes), F32),
                        jnp.zeros((128, 4 * half), F32),
                        jnp.zeros((128, 2 * half), F32),
                    ),
                )
                share = 1.0 / mass
                out_s = out_s * share[:, : 4 * half]
                out_c = out_c * share[:, 4 * half :]
                out_ref[tile * half : (tile + 1) * half, 384 * pair : 384 * pair + 384] = (
                    join_heads(out_s, out_c, half).astype(BF)
                )
                spot = tile * PAIRS + pair
                lse_ref[spot : spot + 1, :] = peak + jnp.log(mass)

    pairs = slots * slot * half * HEADS
    return pl.pallas_call(
        kernel,
        out_shape=(shape(q.shape, BF), shape((2 * PAIRS, lanes), F32)),
        in_specs=[SMEM, VMEM, VMEM, VMEM] + [ANY] * count,
        out_specs=(VMEM, VMEM),
        scratch_shapes=[
            pltpu.VMEM((slots * slot, 1024), BF),
            pltpu.VMEM((slots, slot, lanes), F32),
            pltpu.VMEM((2, slots, slot, half), F32),
            pltpu.SemaphoreType.DMA((4 * nz,)),
        ],
        compiler_params=params(),
        cost_estimate=cost(8 * 256 * pairs, 2 * slots * slot * 1024, pairs),
        name="attend",
    )(ids, q, seg_col, seg_row, *keys)


def attention_backward(q, keys, seg_col, seg_row, attended, grad_att, lse, ids, nz):
    rows = q.shape[0]
    half = rows // 2
    slots = nz + 1
    count = len(keys)
    slot = 2 * half
    lanes = 6 * half

    def kernel(ids_ref, q_ref, col_ref, row_ref, att_ref, grad_ref, lse_ref, *refs):
        key_refs = refs[:count]
        dq_ref, mine_ref, other_ref, kv, dkv, masks, sems = refs[count:]
        fill_masks(nz, half, ids_ref, col_ref, row_ref, masks)
        dkv[...] = jnp.zeros_like(dkv)
        load_keys(nz, half, ids_ref, key_refs, kv, sems)
        for tile in range(2):
            first, end = slot_range(nz, ids_ref, tile)
            for pair in range(PAIRS):
                here = (slice(tile * half, (tile + 1) * half), slice(384 * pair, 384 * pair + 384))
                q_s, q_c = split_heads(q_ref[here], SCALE)
                g_s, g_c = split_heads(grad_ref[here])
                product = grad_ref[here].astype(F32) * att_ref[here].astype(F32)
                turned = [product[:, 128 * k : 128 * k + 128].T for k in range(3)]
                lower = [jnp.sum(t[:64], axis=0, keepdims=True) for t in turned]
                upper = [jnp.sum(t[64:], axis=0, keepdims=True) for t in turned]
                delta = jnp.concatenate(
                    [lower[0], lower[1], upper[1], upper[2], upper[0], lower[2]], axis=1
                )
                spot = tile * PAIRS + pair
                total = lse_ref[spot : spot + 1, :]

                def step(index, carry):
                    dq_s, dq_c = carry
                    at = pl.ds(pl.multiple_of(index * slot, slot), slot)
                    k_lanes = slice(128 * pair, 128 * pair + 128)
                    v_lanes = slice(512 + 128 * pair, 512 + 128 * pair + 128)
                    k, v = kv[at, k_lanes], kv[at, v_lanes]
                    mask = masks[tile, index]
                    s = jnp.concatenate([nt(k, q_s), nt(cross(k), q_c)], axis=1)
                    p = jnp.exp(s + jnp.concatenate([mask] * 6, axis=1) - total)
                    dp = jnp.concatenate([nt(v, g_s), nt(cross(v), g_c)], axis=1)
                    ds = (p * (dp - delta)).astype(BF)
                    p = p.astype(BF)
                    dkv[at, v_lanes] += nn(p[:, : 4 * half], g_s) + cross(
                        nn(p[:, 4 * half :], g_c)
                    )
                    dkv[at, k_lanes] += nn(ds[:, : 4 * half], q_s) + cross(
                        nn(ds[:, 4 * half :], q_c)
                    )
                    k_t = k.T
                    dq_s = dq_s + nn(k_t, ds[:, : 4 * half])
                    dq_c = dq_c + nn(
                        jnp.concatenate([k_t[64:], k_t[:64]], axis=0), ds[:, 4 * half :]
                    )
                    return dq_s, dq_c

                dq_s, dq_c = lax.fori_loop(
                    first,
                    end,
                    step,
                    (jnp.zeros((128, 4 * half), F32), jnp.zeros((128, 2 * half), F32)),
                )
                dq_ref[here] = (SCALE * join_heads(dq_s, dq_c, half)).astype(BF)
        for index in range(slots):
            mine_ref[index] = dkv[index * slot : index * slot + half, :].astype(BF)
            other_ref[index] = dkv[index * slot + half : (index + 1) * slot, :].astype(BF)

    pairs = slots * slot * half * HEADS
    return pl.pallas_call(
        kernel,
        out_shape=(
            shape(q.shape, BF),
            shape((slots, half, 1024), BF),
            shape((slots, half, 1024), BF),
        ),
        in_specs=[SMEM] + [VMEM] * 6 + [ANY] * count,
        out_specs=(VMEM,) * 3,
        scratch_shapes=[
            pltpu.VMEM((slots * slot, 1024), BF),
            pltpu.VMEM((slots * slot, 1024), F32),
            pltpu.VMEM((2, slots, slot, half), F32),
            pltpu.SemaphoreType.DMA((4 * nz,)),
        ],
        compiler_params=params(),
        cost_estimate=cost(20 * 256 * pairs, 2 * slots * slot * 1024, pairs),
        name="attend_back",
    )(ids, q, seg_col, seg_row, attended, grad_att, lse, *keys)


def out_project(tokens, attended, gain, weight, ids, ny, shard):
    rows, width = tokens.shape
    count = len(weight.arrays)

    def kernel(ids_ref, tokens_ref, att_ref, gain_ref, *refs):
        pieces = refs[:count]
        resid_ref, norm_ref, held, sems = refs[count:]
        for copy in start_load(pieces, weight.places, held, sems, ids_ref, ny, shard, width // 2):
            copy.wait()
        resid = tokens_ref[...].astype(F32) + nn(att_ref[...], held[...])
        resid_ref[...] = resid
        norm_ref[...] = (resid * inv_root(resid) * gain_ref[...].astype(F32)).astype(BF)

    return pl.pallas_call(
        kernel,
        out_shape=(shape((rows, width), F32), shape((rows, width), BF)),
        in_specs=[SMEM] + [VMEM] * 3 + [ANY] * count,
        out_specs=(VMEM, VMEM),
        scratch_shapes=[pltpu.VMEM((width, width), BF), pltpu.SemaphoreType.DMA((count,))],
        compiler_params=params(),
        cost_estimate=cost(2 * rows * width * width, 2 * width * width + 10 * rows * width),
        name="out_project",
    )(ids, tokens, attended, gain, *weight.arrays)


def out_back(resid, cotangent, gain, terms, weight, ids, ny, shard):
    rows, width = resid.shape
    count = len(weight.arrays)
    term_count = len(terms)

    def kernel(ids_ref, resid_ref, cot_ref, gain_ref, *refs):
        term_refs, pieces = refs[:term_count], refs[term_count : term_count + count]
        gres_ref, branch_ref, gatt_ref, ggain_ref, held, sems = refs[term_count + count :]
        copies = start_load(pieces, weight.places, held, sems, ids_ref, ny, shard, width // 2)
        grad_norm = term_refs[0][...].astype(F32)
        for ref in term_refs[1:]:
            grad_norm = grad_norm + ref[...].astype(F32)
        resid = resid_ref[...]
        root = inv_root(resid)
        s = resid * root
        ggain_ref[...] = jnp.sum(grad_norm * s, axis=0, keepdims=True)
        t = grad_norm * gain_ref[...].astype(F32)
        gres = cot_ref[...].astype(F32) + root * (
            t - s * jnp.mean(t * s, axis=-1, keepdims=True)
        )
        gres_ref[...] = gres
        branch = gres.astype(BF)
        branch_ref[...] = branch
        for copy in copies:
            copy.wait()
        gatt_ref[...] = nt(branch, held[...]).astype(BF)

    return pl.pallas_call(
        kernel,
        out_shape=(
            shape((rows, width), F32),
            shape((rows, width), BF),
            shape((rows, width), BF),
            shape((1, width), F32),
        ),
        in_specs=[SMEM] + [VMEM] * (3 + term_count) + [ANY] * count,
        out_specs=(VMEM,) * 4,
        scratch_shapes=[pltpu.VMEM((width, width), BF), pltpu.SemaphoreType.DMA((count,))],
        compiler_params=params(),
        cost_estimate=cost(2 * rows * width * width, 2 * width * width + 20 * rows * width),
        name="out_back",
    )(ids, resid, cotangent, gain, *terms, *weight.arrays)


def in_back(tokens, gres, gain, dq, dkv, weight_q, weight_kv, ids, ny, shard):
    rows, width = tokens.shape
    kv_width = dkv.shape[1]
    count_q, count_kv = len(weight_q.arrays), len(weight_kv.arrays)

    def kernel(ids_ref, tokens_ref, gres_ref, gain_ref, dq_ref, dkv_ref, *refs):
        q_pieces, kv_pieces = refs[:count_q], refs[count_q : count_q + count_kv]
        out_ref, ggain_ref, held_q, held_kv, sems_q, sems_kv = refs[count_q + count_kv :]
        copies = start_load(
            kv_pieces, weight_kv.places, held_kv, sems_kv, ids_ref, ny, shard, kv_width // 2
        ) + start_load(q_pieces, weight_q.places, held_q, sems_q, ids_ref, ny, shard, width // 2)
        for copy in copies:
            copy.wait()
        grad_norm = nt(dq_ref[...], held_q[...]) + nt(dkv_ref[...], held_kv[...])
        x = tokens_ref[...].astype(F32)
        root = inv_root(x)
        s = x * root
        ggain_ref[...] = jnp.sum(grad_norm * s, axis=0, keepdims=True)
        t = grad_norm * gain_ref[...].astype(F32)
        out_ref[...] = gres_ref[...] + root * (t - s * jnp.mean(t * s, axis=-1, keepdims=True))

    return pl.pallas_call(
        kernel,
        out_shape=(shape((rows, width), F32), shape((1, width), F32)),
        in_specs=[SMEM] + [VMEM] * 5 + [ANY] * (count_q + count_kv),
        out_specs=(VMEM, VMEM),
        scratch_shapes=[
            pltpu.VMEM((width, width), BF),
            pltpu.VMEM((width, kv_width), BF),
            pltpu.SemaphoreType.DMA((count_q,)),
            pltpu.SemaphoreType.DMA((count_kv,)),
        ],
        compiler_params=params(),
        cost_estimate=cost(
            2 * rows * width * (width + kv_width), 2 * width * (width + kv_width) + 12 * rows * width
        ),
        name="in_back",
    )(ids, tokens, gres, gain, dq, dkv, *weight_q.arrays, *weight_kv.arrays)


def expert_block(normed, cots, coeff, w_gate, w_up, w_down, out_dtype):
    experts, width, units = w_gate.shape
    half = normed[0].shape[0]
    rows = 2 * half

    def kernel(na, nb, ca, cb, coeff_ref, wg_ref, wu_ref, wd_ref, hid_ref, gg_ref, gu_ref,
               mix_ref, gnf_ref, n_all, c_all, mix, gnf):
        e = pl.program_id(0)

        @pl.when(e == 0)
        def _():
            n_all[:half] = na[...]
            n_all[half:] = nb[...]
            c_all[:half] = ca[...]
            c_all[half:] = cb[...]

        wg, wu, wd = wg_ref[0], wu_ref[0], wd_ref[0]
        rows_in, cot = n_all[...], c_all[...]
        lane = lax.broadcasted_iota(jnp.int32, coeff_ref.shape, 1)
        weight = jnp.sum(jnp.where(lane == e, coeff_ref[...], 0.0), axis=1, keepdims=True)
        gate = nn(rows_in, wg)
        up = nn(rows_in, wu)
        back = nt(cot, wd) * weight
        sigma = jax.nn.sigmoid(gate)
        silu = gate * sigma
        hidden = (silu * up * weight).astype(BF)
        grad_gate = (back * up * sigma * (1.0 + gate * (1.0 - sigma))).astype(BF)
        grad_up = (back * silu).astype(BF)
        hid_ref[...] = hidden
        gg_ref[...] = grad_gate
        gu_ref[...] = grad_up
        more = nt(grad_gate, wg) + nt(grad_up, wu)
        out = nn(hidden, wd)

        @pl.when(e == 0)
        def _():
            gnf[...] = more
            mix[...] = out

        @pl.when(e > 0)
        def _():
            gnf[...] += more
            mix[...] += out

        @pl.when(e == experts - 1)
        def _():
            gnf_ref[...] = gnf[...].astype(gnf_ref.dtype)
            mix_ref[...] = mix[...].astype(mix_ref.dtype)

    whole = pl.BlockSpec((half, width), lambda e: (0, 0))
    keep = pl.BlockSpec((rows, width), lambda e: (0, 0))
    unit = pl.BlockSpec((rows, units), lambda e: (0, e))
    return pl.pallas_call(
        kernel,
        grid=(experts,),
        out_shape=(shape((rows, experts * units), BF),) * 3
        + (shape((rows, width), out_dtype),) * 2,
        in_specs=[whole] * 4
        + [
            pl.BlockSpec(coeff.shape, lambda e: (0, 0)),
            pl.BlockSpec((1, width, units), lambda e: (e, 0, 0)),
            pl.BlockSpec((1, width, units), lambda e: (e, 0, 0)),
            pl.BlockSpec((1, units, width), lambda e: (e, 0, 0)),
        ],
        out_specs=(unit, unit, unit, keep, keep),
        scratch_shapes=[pltpu.VMEM((rows, width), BF)] * 2 + [pltpu.VMEM((rows, width), F32)] * 2,
        compiler_params=params(),
        cost_estimate=cost(
            12 * rows * width * experts * units, 6 * experts * width * units + 10 * rows * width
        ),
        name="experts",
    )(*normed, *cots, coeff, w_gate, w_up, w_down)


def expert_grads(first, normed, cots, hidden, grad_gate, grad_up, experts):
    blocks = len(hidden)
    half, width = normed[0].shape
    rows = hidden[0].shape[0]
    units = hidden[0].shape[1] // experts
    pieces = 2 * blocks

    def kernel(first_ref, *refs):
        n_refs, c_refs = refs[:pieces], refs[pieces : 2 * pieces]
        at = 2 * pieces
        h_refs, gg_refs, gu_refs = (
            refs[at : at + blocks],
            refs[at + blocks : at + 2 * blocks],
            refs[at + 2 * blocks : at + 3 * blocks],
        )
        og_ref, ou_ref, od_ref, n_all, c_all, sems = refs[at + 3 * blocks :]

        @pl.when(pl.program_id(0) == 0)
        def _():
            copies = []
            for k in range(pieces):
                to = pl.ds(k * half, half)
                copies.append(pltpu.make_async_copy(n_refs[k], n_all.at[to], sems.at[0, k]))
                copies.append(pltpu.make_async_copy(c_refs[k], c_all.at[to], sems.at[1, k]))
            for copy in copies:
                copy.start()
            for copy in copies:
                copy.wait()

        grads = jnp.concatenate(
            [
                jnp.concatenate([ref[...] for ref in gg_refs], axis=0),
                jnp.concatenate([ref[...] for ref in gu_refs], axis=0),
            ],
            axis=1,
        )
        both = tn(n_all[...], grads)
        og_ref[0] = both[:, :units].astype(BF)
        ou_ref[0] = both[:, units:].astype(BF)
        hid = jnp.concatenate([ref[...] for ref in h_refs], axis=0)
        od_ref[0] = tn(hid, c_all[...]).astype(BF)

    unit = pl.BlockSpec((rows, units), lambda e, first: (0, first[0] + e))
    grid_spec = pltpu.PrefetchScalarGridSpec(
        num_scalar_prefetch=1,
        grid=(experts // 2,),
        in_specs=[ANY] * (2 * pieces) + [unit] * (3 * blocks),
        out_specs=(
            pl.BlockSpec((1, width, units), lambda e, first: (e, 0, 0)),
            pl.BlockSpec((1, width, units), lambda e, first: (e, 0, 0)),
            pl.BlockSpec((1, units, width), lambda e, first: (e, 0, 0)),
        ),
        scratch_shapes=[
            pltpu.VMEM((blocks * rows, width), BF),
            pltpu.VMEM((blocks * rows, width), BF),
            pltpu.SemaphoreType.DMA((2, pieces)),
        ],
    )
    count = experts // 2
    return pl.pallas_call(
        kernel,
        grid_spec=grid_spec,
        out_shape=(
            shape((count, width, units), BF),
            shape((count, width, units), BF),
            shape((count, units, width), BF),
        ),
        compiler_params=params(),
        cost_estimate=cost(
            6 * blocks * rows * width * units * count,
            4 * blocks * rows * width + 6 * count * units * width,
        ),
        name="expert_grads",
    )(first, *normed, *cots, *hidden, *grad_gate, *grad_up)


def spread_halves(mine, beside, core):
    count, a, b = mine.shape

    def kernel(core_ref, mine_ref, beside_ref, out_ref):
        is_mine = pl.program_id(0) // count == core_ref[0]

        @pl.when(is_mine)
        def _():
            out_ref[...] = mine_ref[...].astype(F32)

        @pl.when(jnp.logical_not(is_mine))
        def _():
            out_ref[...] = beside_ref[...].astype(F32)

    block = (1, a, b)
    source = pl.BlockSpec(block, lambda e, core: (lax.rem(e, count), 0, 0))
    return pl.pallas_call(
        kernel,
        grid_spec=pltpu.PrefetchScalarGridSpec(
            num_scalar_prefetch=1,
            grid=(2 * count,),
            in_specs=[source, source],
            out_specs=pl.BlockSpec(block, lambda e, core: (e, 0, 0)),
        ),
        out_shape=shape((2 * count, a, b), F32),
        compiler_params=params(),
        cost_estimate=cost(0, 16 * count * a * b),
        name="spread",
    )(core, mine, beside)


def body(
    tokens,
    segments,
    routes,
    route_weights,
    gain_attn,
    w_query,
    w_key,
    w_value,
    w_out,
    gain_ffn,
    w_gate,
    w_up,
    w_down,
    cotangent,
):
    tokens, cotangent = tokens[0], cotangent[0]
    rows, width = tokens.shape
    half = rows // 2
    nz, ny = lax.axis_size("z"), lax.axis_size("y")
    z, core, y, x = (lax.axis_index(a) for a in ("z", "core", "y", "x"))
    ids = jnp.stack([z, core, y, x]).astype(jnp.int32)
    shard = w_query.shape[0]
    sh = shard // 2
    experts = w_gate.shape[0]
    kv_width = w_key.shape[1] + w_value.shape[1]
    hw = width // 2
    plane = [(dy, dx) for dy in range(ny) for dx in range(2)]
    seg_row = segments
    seg_col = segments.reshape(-1, 1)

    gains = jnp.stack([gain_attn, gain_ffn])
    owners = {}
    for dy, dx in plane:
        got = gains if (dy, dx) == (0, 0) else to_plane(gains, dy, dx)
        owner = lax.rem(y - dy + ny, ny) * 2 + (x if dx == 0 else 1 - x)
        owners[(dy, dx)] = (owner, got)
    slot = jnp.arange(2 * ny, dtype=jnp.int32)[None, :, None]
    all_gains = sum(
        jnp.where(slot == owner, got[:, None, :], jnp.zeros((), BF))
        for owner, got in owners.values()
    ).reshape(2, 1, width)
    gain_a, gain_f = all_gains[0], all_gains[1]

    kv_half = jnp.where(core == 0, w_key, w_value)
    weight_kv = gather_weight(
        [(w_key, 0), (w_value, kv_width // 2)], kv_half[:sh], kv_half[sh:], kv_width // 2
    )

    def column_half(w, row, count):
        return lax.dynamic_slice(w, (row, core * (w.shape[1] // 2)), (count, w.shape[1] // 2))

    weight_q = gather_weight(
        [(w_query, 0)], column_half(w_query, 0, sh), column_half(w_query, sh, sh), hw
    )
    weight_o = gather_weight(
        [(w_out, 0)], column_half(w_out, 0, sh), column_half(w_out, sh, sh), hw
    )

    x_f = tokens.astype(F32)
    normed = (x_f * inv_root(x_f) * gain_a.astype(F32)).astype(BF)
    kv = gathered_matmul(normed, weight_kv, ids, ny, shard, kv_width)
    keys = [kv, swap(kv, "core")]
    for d in range(1, nz):
        low, high = z_move(kv[:half], d), z_move(kv[half:], -d)
        keys += [low, swap(low, "core"), high, swap(high, "core")]
    queries = gathered_matmul(normed, weight_q, ids, ny, shard, width)
    attended, lse = attention_forward(queries, keys, seg_col, seg_row, ids, nz)
    resid, normed_f = out_project(tokens, attended, gain_f, weight_o, ids, ny, shard)

    chosen = routes[0][:, :, None] == jnp.arange(experts, dtype=jnp.int32)[None, None, :]
    coeff = jnp.sum(jnp.where(chosen, route_weights[0][:, :, None], 0.0), axis=1)
    coeffs = {(dy, dx): to_plane(coeff, -dy % ny, dx) for dy, dx in plane if (dy, dx) != (0, 0)}
    coeffs[(0, 0)] = coeff
    cots = plane_gather(cotangent[:half], cotangent[half:])
    cots[(0, 0)] = (cotangent[:half], cotangent[half:])
    norms = plane_gather(normed_f[:half], normed_f[half:])
    norms[(0, 0)] = (normed_f[:half], normed_f[half:])
    order = sorted(plane, key=lambda p: (p[0] != 0) + (p[1] != 0))
    hidden, grad_gate, grad_up, mixes, grad_norms = [], [], [], [], []
    for where in order:
        own = where == (0, 0)
        h, gg, gu, mix, gnf = expert_block(
            norms[where], cots[where], coeffs[where], w_gate, w_up, w_down, F32 if own else BF
        )
        hidden.append(h)
        grad_gate.append(gg)
        grad_up.append(gu)
        mixes.append(mix if own else to_plane(mix, *where))
        grad_norms.append(gnf if own else to_plane(gnf, *where))
    flat_norms = [piece for where in order for piece in norms[where]]
    flat_cots = [piece for where in order for piece in cots[where]]
    count = experts // 2

    def half_grads(which):
        first = (which * count).astype(jnp.int32).reshape(1)
        return expert_grads(first, flat_norms, flat_cots, hidden, grad_gate, grad_up, experts)

    far, near = half_grads(1 - core), half_grads(core)
    expert_totals = []
    for one, two in zip(near, far):
        got = swap(two, "core")
        parts, besides = [], []
        for e in range(count):
            part = z_sum(add_low(one[e], got[e]), z)
            parts.append(part)
            besides.append(swap(part, "core"))
        expert_totals.append(
            spread_halves(
                jnp.stack(parts), jnp.stack(besides), core.astype(jnp.int32).reshape(1)
            )
        )
    result = resid
    for mix in mixes:
        result = result + mix.astype(F32)

    gres, branch, grad_att, ggain_f = out_back(
        resid, cotangent, gain_f, grad_norms, weight_o, ids, ny, shard
    )

    def columns(v, which):
        n = v.shape[1] // 2
        return lax.dynamic_slice(v, (0, which * n), (v.shape[0], n))

    def weight_grad(left, right):
        return tuple(tn(left, columns(right, which)).astype(BF) for which in (core, 1 - core))

    grad_wo = whole_grad(*weight_grad(attended, branch), y, x, z, core)
    dq, dkv_mine, dkv_other = attention_backward(
        queries, keys, seg_col, seg_row, attended, grad_att, lse, ids, nz
    )
    parts = add_low(dkv_mine, swap(dkv_other, "core"))
    low = parts[0].astype(F32)
    high = lax.dynamic_index_in_dim(parts, z + 1, 0, keepdims=False).astype(F32)
    for d in range(1, nz):
        low = low + z_move(parts[d], -d).astype(F32)
        far_high = lax.dynamic_index_in_dim(
            parts, jnp.minimum(z + 1 + d, nz), 0, keepdims=False
        )
        high = high + z_move(far_high, d).astype(F32)
    dkv = jnp.concatenate([low, high], axis=0).astype(BF)
    grad_wq = whole_grad(*weight_grad(normed, dq), y, x, z, core)
    grad_wkv = whole_grad(*weight_grad(normed, dkv), y, x, z, core)
    grad_tokens, ggain_a = in_back(
        tokens, gres, gain_a, dq, dkv, weight_q, weight_kv, ids, ny, shard
    )

    ggains = jnp.concatenate([ggain_a, ggain_f], axis=0)
    ggains = ggains + swap(ggains, "core")
    ggains = ggains.reshape(2, 2 * ny, shard)

    def gain_block(dy, dx):
        place = lax.rem(y + dy, ny) * 2 + (x if dx == 0 else 1 - x)
        return lax.dynamic_index_in_dim(ggains, place, 1, keepdims=False)

    total = gain_block(0, 0)
    for dy, dx in plane[1:]:
        total = total + to_plane(gain_block(dy, dx), dy, dx)
    total = z_sum(total, z)
    kv_cut = w_key.shape[1]
    return (
        result.astype(BF)[None],
        grad_tokens[None],
        total[0],
        grad_wq,
        grad_wkv[:, :kv_cut],
        grad_wkv[:, kv_cut:],
        grad_wo,
        total[1],
        *expert_totals,
    )


def solution(mesh):
    ctx, wt = mesh.shape["ctx"], mesh.shape["wt"]
    fine = Mesh(mesh.devices.reshape(ctx // 2, 2, wt // 2, 2), ("z", "core", "y", "x"))
    c, w = ("z", "core"), ("y", "x")
    rows = P(w, c, None)
    return jax.shard_map(
        body,
        mesh=fine,
        in_specs=(
            rows,
            P(w, None),
            rows,
            rows,
            P(w),
            P(w, None),
            P(w, None),
            P(w, None),
            P(w, None),
            P(w),
            P(None, None, w),
            P(None, None, w),
            P(None, w, None),
            rows,
        ),
        out_specs=(
            rows,
            rows,
            P(w),
            P(w, None),
            P(w, None),
            P(w, None),
            P(w, None),
            P(w),
            P(None, None, w),
            P(None, None, w),
            P(None, w, None),
        ),
        check_vma=False,
    )
```

```python
import jax
import jax.numpy as jnp
from jax import lax
from jax.experimental import pallas as pl
from jax.experimental.pallas import tpu as pltpu
from jax.sharding import Mesh, PartitionSpec as P

HEADS = 24
KV_HEADS = 8
HEAD_DIM = 64
SCALE = HEAD_DIM ** -0.5
PAIRS = KV_HEADS // 2
EPSILON = 1e-06
NEG_LARGE = -1e30
VMEM_BYTES = 56 * 1024 * 1024
BF = jnp.bfloat16
F32 = jnp.float32

VMEM = pl.BlockSpec(memory_space=pltpu.VMEM)
SMEM = pl.BlockSpec(memory_space=pltpu.SMEM)
ANY = pl.BlockSpec(memory_space=pl.ANY)


def params():
    return pltpu.CompilerParams(vmem_limit_bytes=VMEM_BYTES)


def cost(flops, nbytes, trans=0):
    return pl.CostEstimate(flops=int(flops), bytes_accessed=int(nbytes), transcendentals=int(trans))


def shape(dims, dtype):
    return jax.ShapeDtypeStruct(tuple(dims), dtype)


def nn(a, b):
    return lax.dot_general(a, b, (((1,), (0,)), ((), ())), preferred_element_type=F32)


def nt(a, b):
    return lax.dot_general(a, b, (((1,), (1,)), ((), ())), preferred_element_type=F32)


def tn(a, b):
    return lax.dot_general(a, b, (((0,), (0,)), ((), ())), preferred_element_type=F32)


def inv_root(values):
    return lax.rsqrt(jnp.mean(values * values, axis=-1, keepdims=True) + EPSILON)


def swap(v, axis):
    return lax.ppermute(v, axis, [(0, 1), (1, 0)])


def to_y(v, d):
    n = lax.axis_size("y")
    return lax.ppermute(v, "y", [(i, (i + d) % n) for i in range(n)])


def from_y(v, d):
    n = lax.axis_size("y")
    return lax.ppermute(v, "y", [((i + d) % n, i) for i in range(n)])


def to_plane(v, dy, dx):
    n = lax.axis_size("y")
    if dy == 0:
        return swap(v, "x")
    if dx == 0:
        return to_y(v, dy)
    perm = [(2 * i + k, 2 * ((i + dy) % n) + (k ^ dx)) for i in range(n) for k in range(2)]
    return lax.ppermute(v, ("y", "x"), perm)


def z_move(v, d):
    n = lax.axis_size("z")
    return lax.ppermute(v, "z", [(i, i + d) for i in range(n) if 0 <= i + d < n])


def add_low(*terms):
    total = terms[0].astype(F32)
    for term in terms[1:]:
        total = total + term.astype(F32)
    return total.astype(terms[0].dtype)


def z_sum(v, z):
    n = lax.axis_size("z")
    if n == 4:
        inner = add_low(v, lax.ppermute(v, "z", [(0, 1), (3, 2)]))
        whole = add_low(inner, lax.ppermute(inner, "z", [(1, 2), (2, 1)]))
        outer = lax.ppermute(whole, "z", [(1, 0), (2, 3)])
        return jnp.where((z == 0) | (z == 3), outer, whole)
    bit = 1
    while bit < n:
        v = add_low(v, lax.ppermute(v, "z", [(i, i ^ bit) for i in range(n)]))
        bit *= 2
    return v


def plane_reduce(mine, other, y, x):
    n = lax.axis_size("y")
    rows = mine.shape[0] // (2 * n)
    h = rows // 2
    got = swap(other, "core")

    def block(dy, dx, part):
        place = (lax.rem(y + dy, n) * 2 + (x if dx == 0 else 1 - x)) * rows + part * h
        one = lax.dynamic_slice_in_dim(mine, place, h, 0)
        two = lax.dynamic_slice_in_dim(got, place, h, 0)
        return one.astype(F32) + two.astype(F32)

    sent_a = swap(jnp.stack([block(dy, 1, 0) for dy in range(n)]).astype(BF), "x")
    sent_b = [
        to_y(jnp.stack([block(d, 0, 1), block(d, 1, 1)]).astype(BF), d) for d in range(1, n)
    ]
    part_a = [block(dy, 0, 0) + sent_a[dy].astype(F32) for dy in range(n)]
    part_b = [
        block(0, dx, 1) + sum(got_b[dx].astype(F32) for got_b in sent_b) for dx in range(2)
    ]
    total_a = part_a[0]
    for d in range(1, n):
        total_a = total_a + to_y(part_a[d].astype(BF), d).astype(F32)
    total_b = part_b[0] + swap(part_b[1].astype(BF), "x").astype(F32)
    return jnp.concatenate([total_a.astype(BF), total_b.astype(BF)], axis=0)


def whole_grads(mine, other, count, y, x, z, core):
    parts = plane_reduce(mine, other, y, x)
    n = parts.shape[1] // count
    outs = []
    for k in range(count):
        own = z_sum(parts[:, k * n : (k + 1) * n], z)
        beside = swap(own, "core").astype(F32)
        own = own.astype(F32)
        outs.append(
            jnp.where(
                core == 0,
                jnp.concatenate([own, beside], axis=1),
                jnp.concatenate([beside, own], axis=1),
            )
        )
    return outs


class Gathered:
    def __init__(self, arrays, places):
        self.arrays = arrays
        self.places = places


def start_load(refs, places, dst, sems, ids, ny, shard, half_width):
    core, y, x = ids[1], ids[2], ids[3]
    copies = []
    for k, (which, (row0, rows, col0, cols), owner, row, column) in enumerate(places):
        if owner is not None:
            dy, dx = owner
            row = (lax.rem(y + dy, ny) * 2 + (x if dx == 0 else 1 - x)) * shard + row
            row = pl.multiple_of(row, 16)
        if column == "mine":
            column = pl.multiple_of(core * half_width, 128)
        elif column == "other":
            column = pl.multiple_of((1 - core) * half_width, 128)
        copy = pltpu.make_async_copy(
            refs[which].at[pl.ds(row0, rows), pl.ds(col0, cols)],
            dst.at[pl.ds(row, rows), pl.ds(column, cols)],
            sems.at[k],
        )
        copy.start()
        copies.append(copy)
    return copies


def gather_first(w_key, w_value, core):
    ny = lax.axis_size("y")
    rows, cols = w_key.shape
    h = rows // 2
    own = jnp.where(core == 0, w_key, w_value)
    from_x = swap(own, "x")
    pieces, where = [from_x], [((0, 1), 0)]
    sides = [from_y(own, d) for d in range(1, ny)]
    for d, side in enumerate(sides, 1):
        pieces.append(side)
        where.append(((d, 0), 0))
    for d, side in enumerate(sides, 1):
        pieces += [from_y(from_x[:h], d), swap(side[h:], "x")]
        where += [((d, 1), 0), ((d, 1), h)]
    mine = jnp.concatenate(pieces, axis=0)
    other = swap(mine, "core")
    places = [
        (0, (0, rows, 0, cols), (0, 0), 0, 0),
        (1, (0, rows, 0, cols), (0, 0), 0, cols),
    ]
    at = 0
    for piece, (owner, row) in zip(pieces, where):
        count = piece.shape[0]
        places.append((2, (at, count, 0, cols), owner, row, "mine"))
        places.append((3, (at, count, 0, cols), owner, row, "other"))
        at += count
    return Gathered([w_key, w_value, mine, other], places)


def gather_rest(w_query, w_out, core):
    ny = lax.axis_size("y")
    rows, cols = w_query.shape
    n = cols // 2
    half = jnp.concatenate(
        [lax.dynamic_slice(w, (0, core * n), (rows, n)) for w in (w_query, w_out)], axis=1
    )
    gathered = lax.all_gather(half, ("core", "y", "x"), axis=0, tiled=True)
    weights = []
    for k in range(2):
        places = [
            (0, ((c * 2 * ny + w) * rows, rows, k * n, n), None, w * rows, c * n)
            for c in range(2)
            for w in range(2 * ny)
        ]
        weights.append(Gathered([gathered], places))
    return weights


def gathered_matmul(lhs, weight, ids, ny, shard, width):
    count, moves = len(weight.arrays), len(weight.places)
    depth = 2 * ny * shard

    def kernel(ids_ref, lhs_ref, *refs):
        pieces, out_ref, held, sems = refs[:count], refs[count], refs[count + 1], refs[count + 2]
        for copy in start_load(pieces, weight.places, held, sems, ids_ref, ny, shard, width // 2):
            copy.wait()
        out_ref[...] = nn(lhs_ref[...], held[...]).astype(BF)

    return pl.pallas_call(
        kernel,
        out_shape=shape((lhs.shape[0], width), BF),
        in_specs=[SMEM, VMEM] + [ANY] * count,
        out_specs=VMEM,
        scratch_shapes=[pltpu.VMEM((depth, width), BF), pltpu.SemaphoreType.DMA((moves,))],
        compiler_params=params(),
        cost_estimate=cost(2 * lhs.shape[0] * depth * width, 2 * depth * width + 2 * lhs.size),
        name="project",
    )(ids, lhs, *weight.arrays)


def load_keys(nz, half, ids, refs, kv, sems):
    z = ids[0]
    slot = 2 * half

    def place(index, second):
        return kv.at[pl.ds(pl.multiple_of(index * slot + second * half, half), half)]

    copies = []
    for second in range(2):
        own, came = refs[second], refs[2 + second]
        copies.append(pltpu.make_async_copy(own.at[pl.ds(0, half)], place(0, second), sems.at[second, 0]))
        copies.append(
            pltpu.make_async_copy(own.at[pl.ds(half, half)], place(z + 1, second), sems.at[second, nz])
        )
        for d in range(1, nz):
            index = jnp.where(d <= z, d, z + 1 + nz - d)
            copies.append(
                pltpu.make_async_copy(came.at[d - 1], place(index, second), sems.at[second, d])
            )
    for copy in copies:
        copy.start()
    return copies


def slot_range(nz, ids, tile):
    z, core = ids[0], ids[1]
    if tile == 0:
        return 0, z + 1
    last = (z == nz - 1) & (core == 1)
    return jnp.where(last, 0, z + 1), nz + 1


def fill_masks(nz, half, ids, seg_col, seg_row, masks):
    z, core = ids[0], ids[1]
    blocks = 4 * nz
    own = 2 * z + core
    for tile in range(2):
        query_block = own if tile == 0 else blocks - 1 - own
        query_at = pl.multiple_of(query_block * half, half)
        query_seg = seg_row[:, pl.ds(query_at, half)]
        query_pos = query_at + lax.broadcasted_iota(jnp.int32, (1, half), 1)
        first, end = slot_range(nz, ids, tile)

        def fill(index, unused):
            for second in range(2):
                side = core if second == 0 else 1 - core
                key_block = jnp.where(
                    index <= z, 2 * (z - index) + side, blocks - 1 - (2 * (index - 1) + side)
                )
                key_at = pl.multiple_of(key_block * half, half)
                key_seg = seg_col[pl.ds(key_at, half), :]
                key_pos = key_at + lax.broadcasted_iota(jnp.int32, (half, 1), 0)
                allowed = (key_seg == query_seg) & (key_pos <= query_pos)
                masks[tile, index, second * half : (second + 1) * half, :] = jnp.where(
                    allowed, 0.0, NEG_LARGE
                )
            return unused

        lax.fori_loop(first, end, fill, 0)


def split_heads(tile_rows, scale=None):
    half = tile_rows.shape[0]
    if scale is not None:
        tile_rows = tile_rows * jnp.asarray(scale, tile_rows.dtype)
    lane = lax.broadcasted_iota(jnp.int32, (half, 128), 1)
    zero = jnp.zeros((half, 128), tile_rows.dtype)
    t0, t1, t2 = (tile_rows[:, 128 * k : 128 * k + 128] for k in range(3))

    def low(t):
        return jnp.where(lane < 64, t, zero)

    def high(t):
        return jnp.where(lane >= 64, t, zero)

    straight = jnp.concatenate([low(t0), low(t1), high(t1), high(t2)], axis=0)
    crossed = jnp.concatenate([high(t0), low(t2)], axis=0)
    return straight, crossed


def join_heads(straight_t, crossed_t, half):
    def head(t, k, upper):
        return t[64 * upper : 64 * upper + 64, half * k : half * k + half]

    tiles = (
        (head(straight_t, 0, 0), head(crossed_t, 0, 1)),
        (head(straight_t, 1, 0), head(straight_t, 2, 1)),
        (head(crossed_t, 1, 0), head(straight_t, 3, 1)),
    )
    return jnp.concatenate([jnp.concatenate(t, axis=0).T for t in tiles], axis=1)


def cross(v):
    return jnp.concatenate([v[:, 64:], v[:, :64]], axis=1)


def attention_forward(q, keys, seg_col, seg_row, ids, nz):
    rows = q.shape[0]
    half = rows // 2
    slots = nz + 1
    count = len(keys)
    slot = 2 * half
    lanes = 6 * half

    def kernel(ids_ref, q_ref, col_ref, row_ref, *refs):
        key_refs = refs[:count]
        out_ref, lse_ref, kv, scores, masks, sems = refs[count:]
        copies = load_keys(nz, half, ids_ref, key_refs, kv, sems)
        fill_masks(nz, half, ids_ref, col_ref, row_ref, masks)
        for copy in copies:
            copy.wait()
        for tile in range(2):
            first, end = slot_range(nz, ids_ref, tile)
            for pair in range(PAIRS):
                straight, crossed = split_heads(
                    q_ref[tile * half : (tile + 1) * half, 384 * pair : 384 * pair + 384], SCALE
                )

                def score(index, peak):
                    at = pl.ds(pl.multiple_of(index * slot, slot), slot)
                    k = kv[at, 128 * pair : 128 * pair + 128]
                    mask = masks[tile, index]
                    s = jnp.concatenate([nt(k, straight), nt(cross(k), crossed)], axis=1)
                    s = s + jnp.concatenate([mask] * 6, axis=1)
                    scores[index] = s
                    return jnp.maximum(peak, jnp.max(s, axis=0, keepdims=True))

                peak = lax.fori_loop(
                    first, end, score, jnp.full((1, lanes), NEG_LARGE, F32)
                )

                def mix(index, carry):
                    mass, out_s, out_c = carry
                    at = pl.ds(pl.multiple_of(index * slot, slot), slot)
                    v = kv[at, 512 + 128 * pair : 512 + 128 * pair + 128]
                    p = jnp.exp(scores[index] - peak)
                    mass = mass + jnp.sum(p, axis=0, keepdims=True)
                    p = p.astype(BF)
                    v_t = v.T
                    out_s = out_s + nn(v_t, p[:, : 4 * half])
                    out_c = out_c + nn(
                        jnp.concatenate([v_t[64:], v_t[:64]], axis=0), p[:, 4 * half :]
                    )
                    return mass, out_s, out_c

                mass, out_s, out_c = lax.fori_loop(
                    first,
                    end,
                    mix,
                    (
                        jnp.zeros((1, lanes), F32),
                        jnp.zeros((128, 4 * half), F32),
                        jnp.zeros((128, 2 * half), F32),
                    ),
                )
                share = 1.0 / mass
                out_s = out_s * share[:, : 4 * half]
                out_c = out_c * share[:, 4 * half :]
                out_ref[tile * half : (tile + 1) * half, 384 * pair : 384 * pair + 384] = (
                    join_heads(out_s, out_c, half).astype(BF)
                )
                spot = tile * PAIRS + pair
                lse_ref[spot : spot + 1, :] = peak + jnp.log(mass)

    pairs = slots * slot * half * HEADS
    return pl.pallas_call(
        kernel,
        out_shape=(shape(q.shape, BF), shape((2 * PAIRS, lanes), F32)),
        in_specs=[SMEM, VMEM, VMEM, VMEM] + [ANY] * count,
        out_specs=(VMEM, VMEM),
        scratch_shapes=[
            pltpu.VMEM((slots * slot, 1024), BF),
            pltpu.VMEM((slots, slot, lanes), F32),
            pltpu.VMEM((2, slots, slot, half), F32),
            pltpu.SemaphoreType.DMA((2, nz + 1)),
        ],
        compiler_params=params(),
        cost_estimate=cost(8 * 256 * pairs, 2 * slots * slot * 1024, pairs),
        name="attend",
    )(ids, q, seg_col, seg_row, *keys)


def attention_backward(q, keys, seg_col, seg_row, attended, grad_att, lse, ids, nz):
    rows = q.shape[0]
    half = rows // 2
    slots = nz + 1
    count = len(keys)
    slot = 2 * half
    lanes = 6 * half

    def kernel(ids_ref, q_ref, col_ref, row_ref, att_ref, grad_ref, lse_ref, *refs):
        key_refs = refs[:count]
        dq_ref, mine_ref, other_ref, kv, dkv, masks, sems = refs[count:]
        copies = load_keys(nz, half, ids_ref, key_refs, kv, sems)
        fill_masks(nz, half, ids_ref, col_ref, row_ref, masks)
        dkv[...] = jnp.zeros_like(dkv)
        for copy in copies:
            copy.wait()
        for tile in range(2):
            first, end = slot_range(nz, ids_ref, tile)
            for pair in range(PAIRS):
                here = (slice(tile * half, (tile + 1) * half), slice(384 * pair, 384 * pair + 384))
                q_s, q_c = split_heads(q_ref[here], SCALE)
                g_s, g_c = split_heads(grad_ref[here])
                product = grad_ref[here].astype(F32) * att_ref[here].astype(F32)
                turned = [product[:, 128 * k : 128 * k + 128].T for k in range(3)]
                lower = [jnp.sum(t[:64], axis=0, keepdims=True) for t in turned]
                upper = [jnp.sum(t[64:], axis=0, keepdims=True) for t in turned]
                delta = jnp.concatenate(
                    [lower[0], lower[1], upper[1], upper[2], upper[0], lower[2]], axis=1
                )
                spot = tile * PAIRS + pair
                total = lse_ref[spot : spot + 1, :]

                def step(index, carry):
                    dq_s, dq_c = carry
                    at = pl.ds(pl.multiple_of(index * slot, slot), slot)
                    k_lanes = slice(128 * pair, 128 * pair + 128)
                    v_lanes = slice(512 + 128 * pair, 512 + 128 * pair + 128)
                    k, v = kv[at, k_lanes], kv[at, v_lanes]
                    mask = masks[tile, index]
                    s = jnp.concatenate([nt(k, q_s), nt(cross(k), q_c)], axis=1)
                    p = jnp.exp(s + jnp.concatenate([mask] * 6, axis=1) - total)
                    dp = jnp.concatenate([nt(v, g_s), nt(cross(v), g_c)], axis=1)
                    ds = (p * (dp - delta)).astype(BF)
                    p = p.astype(BF)
                    dkv[at, v_lanes] += nn(p[:, : 4 * half], g_s) + cross(
                        nn(p[:, 4 * half :], g_c)
                    )
                    dkv[at, k_lanes] += nn(ds[:, : 4 * half], q_s) + cross(
                        nn(ds[:, 4 * half :], q_c)
                    )
                    k_t = k.T
                    dq_s = dq_s + nn(k_t, ds[:, : 4 * half])
                    dq_c = dq_c + nn(
                        jnp.concatenate([k_t[64:], k_t[:64]], axis=0), ds[:, 4 * half :]
                    )
                    return dq_s, dq_c

                dq_s, dq_c = lax.fori_loop(
                    first,
                    end,
                    step,
                    (jnp.zeros((128, 4 * half), F32), jnp.zeros((128, 2 * half), F32)),
                )
                dq_ref[here] = (SCALE * join_heads(dq_s, dq_c, half)).astype(BF)
        for index in range(slots):
            mine_ref[index] = dkv[index * slot : index * slot + half, :].astype(BF)
            other_ref[index] = dkv[index * slot + half : (index + 1) * slot, :].astype(BF)

    pairs = slots * slot * half * HEADS
    return pl.pallas_call(
        kernel,
        out_shape=(
            shape(q.shape, BF),
            shape((slots, half, 1024), BF),
            shape((slots, half, 1024), BF),
        ),
        in_specs=[SMEM] + [VMEM] * 6 + [ANY] * count,
        out_specs=(VMEM,) * 3,
        scratch_shapes=[
            pltpu.VMEM((slots * slot, 1024), BF),
            pltpu.VMEM((slots * slot, 1024), F32),
            pltpu.VMEM((2, slots, slot, half), F32),
            pltpu.SemaphoreType.DMA((2, nz + 1)),
        ],
        compiler_params=params(),
        cost_estimate=cost(300 * 256 * pairs, 2 * slots * slot * 1024, pairs),
        name="attend_back",
    )(ids, q, seg_col, seg_row, attended, grad_att, lse, *keys)


def out_project(tokens, attended, gain, weight, ids, ny, shard):
    rows, width = tokens.shape
    count, moves = len(weight.arrays), len(weight.places)

    def kernel(ids_ref, tokens_ref, att_ref, gain_ref, *refs):
        pieces = refs[:count]
        resid_ref, norm_ref, held, sems = refs[count:]
        for copy in start_load(pieces, weight.places, held, sems, ids_ref, ny, shard, width // 2):
            copy.wait()
        resid = tokens_ref[...].astype(F32) + nn(att_ref[...], held[...])
        resid_ref[...] = resid
        norm_ref[...] = (resid * inv_root(resid) * gain_ref[...]).astype(BF)

    return pl.pallas_call(
        kernel,
        out_shape=(shape((rows, width), F32), shape((rows, width), BF)),
        in_specs=[SMEM] + [VMEM] * 3 + [ANY] * count,
        out_specs=(VMEM, VMEM),
        scratch_shapes=[pltpu.VMEM((width, width), BF), pltpu.SemaphoreType.DMA((moves,))],
        compiler_params=params(),
        cost_estimate=cost(2 * rows * width * width, 2 * width * width + 10 * rows * width),
        name="out_project",
    )(ids, tokens, attended, gain, *weight.arrays)


def out_back(resid, cotangent, gain, terms, weight, ids, ny, shard, after=()):
    rows, width = resid.shape
    count, moves = len(weight.arrays), len(weight.places)
    term_count = len(terms)

    def kernel(ids_ref, resid_ref, cot_ref, gain_ref, *refs):
        term_refs, pieces = refs[:term_count], refs[term_count : term_count + count]
        gres_ref, branch_ref, gatt_ref, ggain_ref, held, sems = refs[term_count + count + len(after) :]
        copies = start_load(pieces, weight.places, held, sems, ids_ref, ny, shard, width // 2)
        grad_norm = term_refs[0][...].astype(F32)
        for ref in term_refs[1:]:
            grad_norm = grad_norm + ref[...].astype(F32)
        resid = resid_ref[...]
        root = inv_root(resid)
        s = resid * root
        ggain_ref[...] = jnp.sum(grad_norm * s, axis=0, keepdims=True)
        t = grad_norm * gain_ref[...]
        gres = cot_ref[...].astype(F32) + root * (
            t - s * jnp.mean(t * s, axis=-1, keepdims=True)
        )
        gres_ref[...] = gres
        branch = gres.astype(BF)
        branch_ref[...] = branch
        for copy in copies:
            copy.wait()
        gatt_ref[...] = nt(branch, held[...]).astype(BF)

    return pl.pallas_call(
        kernel,
        out_shape=(
            shape((rows, width), F32),
            shape((rows, width), BF),
            shape((rows, width), BF),
            shape((1, width), F32),
        ),
        in_specs=[SMEM] + [VMEM] * (3 + term_count) + [ANY] * (count + len(after)),
        out_specs=(VMEM,) * 4,
        scratch_shapes=[pltpu.VMEM((width, width), BF), pltpu.SemaphoreType.DMA((moves,))],
        compiler_params=params(),
        cost_estimate=cost(2 * rows * width * width, 2 * width * width + 20 * rows * width),
        name="out_back",
    )(ids, resid, cotangent, gain, *terms, *weight.arrays, *after)


def in_back(tokens, gres, gain, dq, dkv, weight_q, weight_kv, ids, ny, shard, after=()):
    rows, width = tokens.shape
    kv_width = dkv.shape[1]
    count_q, count_kv = len(weight_q.arrays), len(weight_kv.arrays)

    def kernel(ids_ref, tokens_ref, gres_ref, gain_ref, dq_ref, dkv_ref, *refs):
        q_pieces, kv_pieces = refs[:count_q], refs[count_q : count_q + count_kv]
        out_ref, ggain_ref, held_q, held_kv, sems_q, sems_kv = refs[count_q + count_kv + len(after) :]
        copies = start_load(
            kv_pieces, weight_kv.places, held_kv, sems_kv, ids_ref, ny, shard, kv_width // 2
        ) + start_load(q_pieces, weight_q.places, held_q, sems_q, ids_ref, ny, shard, width // 2)
        for copy in copies:
            copy.wait()
        grad_norm = nt(dq_ref[...], held_q[...]) + nt(dkv_ref[...], held_kv[...])
        x = tokens_ref[...].astype(F32)
        root = inv_root(x)
        s = x * root
        ggain_ref[...] = jnp.sum(grad_norm * s, axis=0, keepdims=True)
        t = grad_norm * gain_ref[...]
        out_ref[...] = gres_ref[...] + root * (t - s * jnp.mean(t * s, axis=-1, keepdims=True))

    return pl.pallas_call(
        kernel,
        out_shape=(shape((rows, width), F32), shape((1, width), F32)),
        in_specs=[SMEM] + [VMEM] * 5 + [ANY] * (count_q + count_kv + len(after)),
        out_specs=(VMEM, VMEM),
        scratch_shapes=[
            pltpu.VMEM((width, width), BF),
            pltpu.VMEM((width, kv_width), BF),
            pltpu.SemaphoreType.DMA((len(weight_q.places),)),
            pltpu.SemaphoreType.DMA((len(weight_kv.places),)),
        ],
        compiler_params=params(),
        cost_estimate=cost(
            2 * rows * width * (width + kv_width), 2 * width * (width + kv_width) + 12 * rows * width
        ),
        name="in_back",
    )(ids, tokens, gres, gain, dq, dkv, *weight_q.arrays, *weight_kv.arrays, *after)


def expert_block(block_ids, blocks, cot_all, coeffs, w_gate, w_up, w_down, out_dtype, after=()):
    experts, width, units = w_gate.shape
    pieces = [p for block in blocks for p in block]
    count, many, extra = len(pieces), len(blocks), len(after)
    size = coeffs[0].shape[0]
    rows = many * size

    def kernel(id_ref, *refs):
        n_refs, refs = refs[:count], refs[count:]
        c_refs, refs = refs[:many], refs[many:]
        (coeff_ref, wg_ref, wu_ref, wd_ref), refs = refs[:4], refs[4 + extra :]
        (hid_ref, gg_ref, gu_ref), refs = refs[:3], refs[3:]
        mix_refs, gnf_refs, (mix, gnf) = refs[:many], refs[many : 2 * many], refs[2 * many :]
        e = pl.program_id(0)
        wg, wu, wd = wg_ref[0], wu_ref[0], wd_ref[0]
        rows_in = jnp.concatenate([ref[...] for ref in n_refs], axis=0)
        cot = jnp.concatenate([ref[...] for ref in c_refs], axis=0)
        lane = lax.broadcasted_iota(jnp.int32, coeff_ref.shape, 1)
        weight = jnp.sum(jnp.where(lane == e, coeff_ref[...], 0.0), axis=1, keepdims=True)
        gate = nn(rows_in, wg)
        up = nn(rows_in, wu)
        back = nt(cot, wd) * weight
        sigma = jax.nn.sigmoid(gate)
        silu = gate * sigma
        hidden = (silu * up * weight).astype(BF)
        grad_gate = (back * up * sigma * (1.0 + gate * (1.0 - sigma))).astype(BF)
        grad_up = (back * silu).astype(BF)
        hid_ref[...] = hidden
        gg_ref[...] = grad_gate
        gu_ref[...] = grad_up
        more = nt(grad_gate, wg) + nt(grad_up, wu)
        out = nn(hidden, wd)

        @pl.when(e == 0)
        def _():
            gnf[...] = more
            mix[...] = out

        @pl.when(e > 0)
        def _():
            gnf[...] += more
            mix[...] += out

        @pl.when(e == experts - 1)
        def _():
            for k in range(many):
                here = slice(k * size, (k + 1) * size)
                gnf_refs[k][...] = gnf[here].astype(out_dtype)
                mix_refs[k][...] = mix[here].astype(out_dtype)

    keep = pl.BlockSpec((size, width), lambda e, s: (0, 0))
    unit = pl.BlockSpec((rows, units), lambda e, s: (0, e))
    outs = pl.pallas_call(
        kernel,
        grid_spec=pltpu.PrefetchScalarGridSpec(
            num_scalar_prefetch=1,
            grid=(experts,),
            in_specs=[pl.BlockSpec(p.shape, lambda e, s: (0, 0)) for p in pieces]
            + [pl.BlockSpec((size, width), lambda e, s, k=k: (s[k], 0)) for k in range(many)]
            + [
                pl.BlockSpec((rows, experts), lambda e, s: (0, 0)),
                pl.BlockSpec((1, width, units), lambda e, s: (e, 0, 0)),
                pl.BlockSpec((1, width, units), lambda e, s: (e, 0, 0)),
                pl.BlockSpec((1, units, width), lambda e, s: (e, 0, 0)),
            ]
            + [ANY] * extra,
            out_specs=(unit,) * 3 + (keep,) * (2 * many),
            scratch_shapes=[pltpu.VMEM((rows, width), F32)] * 2,
        ),
        out_shape=(shape((rows, experts * units), BF),) * 3
        + (shape((size, width), out_dtype),) * (2 * many),
        compiler_params=params(),
        cost_estimate=cost(
            12 * rows * width * experts * units, 6 * experts * width * units + 10 * rows * width
        ),
        name="experts",
    )(
        block_ids,
        *pieces,
        *[cot_all] * many,
        jnp.concatenate(coeffs, axis=0),
        w_gate,
        w_up,
        w_down,
        *after,
    )
    return outs[:3], outs[3 : 3 + many], outs[3 + many :]


def expert_grads(block_ids, pieces, cot_all, hidden, grad_gate, grad_up, experts, size):
    groups = len(hidden)
    width = cot_all.shape[1]
    units = hidden[0].shape[1] // experts
    count = len(pieces)
    blocks = block_ids.shape[0]
    rows = blocks * size

    def kernel(id_ref, *refs):
        n_refs, c_ref = refs[:count], refs[count]
        at = count + 1
        h_refs, gg_refs, gu_refs = (
            refs[at : at + groups],
            refs[at + groups : at + 2 * groups],
            refs[at + 2 * groups : at + 3 * groups],
        )
        out_ref, n_all, c_all, n_sems, c_sems = refs[at + 3 * groups :]

        @pl.when(pl.program_id(0) == 0)
        def _():
            copies, row = [], 0
            for k, ref in enumerate(n_refs):
                copies.append(
                    pltpu.make_async_copy(ref, n_all.at[pl.ds(row, ref.shape[0])], n_sems.at[k])
                )
                row += ref.shape[0]
            for k in range(blocks):
                start = pl.multiple_of(id_ref[k] * size, size)
                copies.append(
                    pltpu.make_async_copy(
                        c_ref.at[pl.ds(start, size)], c_all.at[pl.ds(k * size, size)], c_sems.at[k]
                    )
                )
            for copy in copies:
                copy.start()
            for copy in copies:
                copy.wait()

        grads = jnp.concatenate(
            [
                jnp.concatenate([ref[...] for ref in gg_refs], axis=0),
                jnp.concatenate([ref[...] for ref in gu_refs], axis=0),
            ],
            axis=1,
        )
        out_ref[:, : 2 * units] = tn(n_all[...], grads).astype(BF)
        hid = jnp.concatenate([ref[...] for ref in h_refs], axis=0)
        out_ref[:, 2 * units :] = tn(c_all[...], hid).astype(BF)

    grid_spec = pltpu.PrefetchScalarGridSpec(
        num_scalar_prefetch=1,
        grid=(experts,),
        in_specs=[ANY] * (count + 1)
        + [
            pl.BlockSpec((one.shape[0], units), lambda e, s: (0, e))
            for group in (hidden, grad_gate, grad_up)
            for one in group
        ],
        out_specs=pl.BlockSpec((width, 3 * units), lambda e, s: (e, 0)),
        scratch_shapes=[
            pltpu.VMEM((rows, width), BF),
            pltpu.VMEM((rows, width), BF),
            pltpu.SemaphoreType.DMA((count,)),
            pltpu.SemaphoreType.DMA((blocks,)),
        ],
    )
    return pl.pallas_call(
        kernel,
        grid_spec=grid_spec,
        out_shape=shape((experts * width, 3 * units), BF),
        compiler_params=params(),
        cost_estimate=cost(
            6 * rows * width * units * experts, 4 * rows * width + 6 * experts * units * width
        ),
        name="expert_grads",
    )(block_ids, *pieces, cot_all, *hidden, *grad_gate, *grad_up)


def spread_grads(grads, experts):
    width, units = grads.shape[0] // experts, grads.shape[1] // 3

    def kernel(in_ref, gate_ref, up_ref, down_ref):
        gate_ref[0] = in_ref[:, :units].astype(F32)
        up_ref[0] = in_ref[:, units : 2 * units].astype(F32)
        down_ref[0] = in_ref[:, 2 * units :].astype(F32).T

    side = pl.BlockSpec((1, width, units), lambda e: (e, 0, 0))
    return pl.pallas_call(
        kernel,
        grid=(experts,),
        out_shape=(shape((experts, width, units), F32),) * 2
        + (shape((experts, units, width), F32),),
        in_specs=[pl.BlockSpec((width, 3 * units), lambda e: (e, 0))],
        out_specs=(side, side, pl.BlockSpec((1, units, width), lambda e: (e, 0, 0))),
        compiler_params=params(),
        cost_estimate=cost(0, 6 * grads.size),
        name="spread_grads",
    )(grads)


def weight_grads(ids, pairs, after=()):
    depth = pairs[0][0].shape[1]
    halves = [right.shape[1] // 2 for _, right in pairs]
    width = sum(halves)
    rows = pairs[0][0].shape[0]

    def kernel(ids_ref, *refs):
        mine_ref, other_ref = refs[2 * len(pairs) + len(after) :]
        core, at = ids_ref[1], 0
        for k, n in enumerate(halves):
            left, right = refs[2 * k][...], refs[2 * k + 1]
            for out_ref, side in ((mine_ref, core), (other_ref, 1 - core)):
                columns = right[:, pl.ds(pl.multiple_of(side * n, 128), n)]
                out_ref[:, at : at + n] = tn(left, columns).astype(BF)
            at += n

    return pl.pallas_call(
        kernel,
        out_shape=(shape((depth, width), BF),) * 2,
        in_specs=[SMEM] + [VMEM] * (2 * len(pairs)) + [ANY] * len(after),
        out_specs=(VMEM,) * 2,
        compiler_params=params(),
        cost_estimate=cost(4 * rows * depth * width, 4 * depth * width),
        name="weight_grads",
    )(ids, *[v for pair in pairs for v in pair], *after)


def body(
    tokens,
    segments,
    routes,
    route_weights,
    gain_attn,
    w_query,
    w_key,
    w_value,
    w_out,
    gain_ffn,
    w_gate,
    w_up,
    w_down,
    cotangent,
):
    tokens, cotangent = tokens[0], cotangent[0]
    rows, width = tokens.shape
    half = rows // 2
    nz, ny = lax.axis_size("z"), lax.axis_size("y")
    z, core, y, x = (lax.axis_index(a) for a in ("z", "core", "y", "x"))
    ids = jnp.stack([z, core, y, x]).astype(jnp.int32)
    shard = w_query.shape[0]
    experts = w_gate.shape[0]
    kv_width = w_key.shape[1] + w_value.shape[1]
    plane = [(dy, dx) for dy in range(ny) for dx in range(2)]
    seg_row = segments
    seg_col = segments.reshape(-1, 1)

    chosen = routes[0][:, :, None] == jnp.arange(experts, dtype=jnp.int32)[None, None, :]
    coeff = jnp.sum(jnp.where(chosen, route_weights[0][:, :, None], 0.0), axis=1)
    small = jnp.concatenate(
        [coeff.reshape(-1), gain_attn.astype(F32), gain_ffn.astype(F32)]
    ).reshape(-1, 128)
    coeffs = {}
    slot = jnp.arange(2 * ny, dtype=jnp.int32)[None, :, None]
    gains = jnp.zeros((2, 2 * ny, shard), F32)
    owners = {}
    for dy, dx in plane:
        got = small if (dy, dx) == (0, 0) else to_plane(small, -dy % ny, dx)
        got = got.reshape(-1)
        owner = lax.rem(y + dy, ny) * 2 + (x if dx == 0 else 1 - x)
        owners[(dy, dx)] = owner.astype(jnp.int32).reshape(1)
        coeffs[(dy, dx)] = got[: rows * experts].reshape(rows, experts)
        pair = got[rows * experts :].reshape(2, 1, shard)
        gains = gains + jnp.where(slot == owner, pair, 0.0)
    gain_a, gain_f = gains[0].reshape(1, width), gains[1].reshape(1, width)

    weight_kv = gather_first(w_key, w_value, core)
    weight_q, weight_o = gather_rest(w_query, w_out, core)
    cot_all = lax.all_gather(cotangent, ("y", "x"), axis=0, tiled=True)

    x_f = tokens.astype(F32)
    normed = (x_f * inv_root(x_f) * gain_a).astype(BF)
    kv = gathered_matmul(normed, weight_kv, ids, ny, shard, kv_width)
    beside = swap(kv, "core")
    came = []
    for d in range(1, nz):
        start = jnp.where(z + d < nz, 0, half)
        piece = lax.dynamic_slice_in_dim(kv, start, half, 0)
        came.append(lax.ppermute(piece, "z", [(i, (i + d) % nz) for i in range(nz)]))
    came = jnp.stack(came)
    keys = [kv, beside, came, swap(came, "core")]
    queries = gathered_matmul(normed, weight_q, ids, ny, shard, width)
    attended, lse = attention_forward(queries, keys, seg_col, seg_row, ids, nz)
    resid, normed_f = out_project(tokens, attended, gain_f, weight_o, ids, ny, shard)

    from_x = swap(normed_f, "x")
    norms = {(0, 0): [normed_f], (0, 1): [from_x]}
    for d in range(1, ny):
        side = from_y(normed_f, d)
        norms[(d, 0)] = [side]
        norms[(d, 1)] = [from_y(from_x[:half], d), swap(side[half:], "x")]
    groups = [
        [(0, 0)],
        [(0, 1)] + [(d, 0) for d in range(1, ny)],
        [(d, 1) for d in range(1, ny)],
    ]
    hidden, grad_gate, grad_up, mixes, grad_norms, after = [], [], [], [], [], ()
    for group in groups:
        own = group == [(0, 0)]
        (h, gg, gu), mix, gnf = expert_block(
            jnp.concatenate([owners[where] for where in group]),
            [norms[where] for where in group],
            cot_all,
            [coeffs[where] for where in group],
            w_gate,
            w_up,
            w_down,
            F32 if own else BF,
            after,
        )
        after = (h,)
        hidden.append(h)
        grad_gate.append(gg)
        grad_up.append(gu)
        for where, one, two in zip(group, mix, gnf):
            mixes.append(one if own else to_plane(one, *where))
            grad_norms.append(two if own else to_plane(two, *where))
    order = [where for group in groups for where in group]
    expert_parts = expert_grads(
        jnp.concatenate([owners[where] for where in order]),
        [piece for where in order for piece in norms[where]],
        cot_all,
        hidden,
        grad_gate,
        grad_up,
        experts,
        rows,
    )
    expert_shard = lax.psum_scatter(
        expert_parts, ("z", "core"), scatter_dimension=0, tiled=True
    )
    result = resid
    for mix in mixes:
        result = result + mix.astype(F32)
    result = result.astype(BF)

    gres, branch, grad_att, ggain_f = out_back(
        resid, cotangent, gain_f, grad_norms, weight_o, ids, ny, shard, (expert_parts,)
    )
    dq, dkv_mine, dkv_other = attention_backward(
        queries, keys, seg_col, seg_row, attended, grad_att, lse, ids, nz
    )
    oq = weight_grads(ids, [(attended, branch), (normed, dq)])
    dkv_mine = lax.optimization_barrier((dkv_mine, oq[0]))[0]
    parts = add_low(dkv_mine, swap(dkv_other, "core"))
    low = parts[0].astype(F32)
    high = lax.dynamic_index_in_dim(parts, z + 1, 0, keepdims=False).astype(F32)
    for d in range(1, nz):
        index = jnp.where(d <= z, d, z + 1 + nz - d)
        piece = lax.dynamic_index_in_dim(parts, index, 0, keepdims=False)
        got = lax.ppermute(piece, "z", [((i + d) % nz, i) for i in range(nz)]).astype(F32)
        low = low + jnp.where(z + d < nz, got, 0.0)
        high = high + jnp.where(z + d < nz, 0.0, got)
    dkv = jnp.concatenate([low, high], axis=0).astype(BF)
    expert_shard = lax.optimization_barrier((expert_shard, dkv))[0]
    expert_totals = spread_grads(
        lax.all_gather(expert_shard, ("z", "core"), axis=0, tiled=True), experts
    )
    grad_wo, grad_wq = whole_grads(*oq, 2, y, x, z, core)
    (grad_wkv,) = whole_grads(*weight_grads(ids, [(normed, dkv)]), 1, y, x, z, core)
    grad_tokens, ggain_a = in_back(
        tokens, gres, gain_a, dq, dkv, weight_q, weight_kv, ids, ny, shard, (result,)
    )

    ggains = jnp.concatenate([ggain_a, ggain_f], axis=0)
    ggains = ggains + swap(ggains, "core")
    ggains = ggains.reshape(2, 2 * ny, shard)

    def gain_block(dy, dx):
        place = lax.rem(y + dy, ny) * 2 + (x if dx == 0 else 1 - x)
        return lax.dynamic_index_in_dim(ggains, place, 1, keepdims=False)

    total = gain_block(0, 0)
    for dy, dx in plane[1:]:
        total = total + to_plane(gain_block(dy, dx), dy, dx)
    total = z_sum(total, z)
    kv_cut = w_key.shape[1]
    return (
        result[None],
        grad_tokens[None],
        total[0],
        grad_wq,
        grad_wkv[:, :kv_cut],
        grad_wkv[:, kv_cut:],
        grad_wo,
        total[1],
        *expert_totals,
    )


def solution(mesh):
    ctx, wt = mesh.shape["ctx"], mesh.shape["wt"]
    fine = Mesh(mesh.devices.reshape(ctx // 2, 2, wt // 2, 2), ("z", "core", "y", "x"))
    c, w = ("z", "core"), ("y", "x")
    rows = P(w, c, None)
    return jax.shard_map(
        body,
        mesh=fine,
        in_specs=(
            rows,
            P(w, None),
            rows,
            rows,
            P(w),
            P(w, None),
            P(w, None),
            P(w, None),
            P(w, None),
            P(w),
            P(None, None, w),
            P(None, None, w),
            P(None, w, None),
            rows,
        ),
        out_specs=(
            rows,
            rows,
            P(w),
            P(w, None),
            P(w, None),
            P(w, None),
            P(w, None),
            P(w),
            P(None, None, w),
            P(None, None, w),
            P(None, w, None),
        ),
        check_vma=False,
    )
```

```python
import jax
import jax.numpy as jnp
from jax import lax
from jax.experimental import pallas as pl
from jax.experimental.pallas import tpu as pltpu
from jax.sharding import Mesh, PartitionSpec as P

HEADS = 24
KV_HEADS = 8
HEAD_DIM = 64
SCALE = HEAD_DIM ** -0.5
PAIRS = KV_HEADS // 2
EPSILON = 1e-06
NEG_LARGE = -1e30
VMEM_BYTES = 56 * 1024 * 1024
BF = jnp.bfloat16
F32 = jnp.float32

VMEM = pl.BlockSpec(memory_space=pltpu.VMEM)
SMEM = pl.BlockSpec(memory_space=pltpu.SMEM)
ANY = pl.BlockSpec(memory_space=pl.ANY)


def params():
    return pltpu.CompilerParams(vmem_limit_bytes=VMEM_BYTES)


def cost(flops, nbytes, trans=0):
    return pl.CostEstimate(flops=int(flops), bytes_accessed=int(nbytes), transcendentals=int(trans))


def shape(dims, dtype):
    return jax.ShapeDtypeStruct(tuple(dims), dtype)


def nn(a, b):
    return lax.dot_general(a, b, (((1,), (0,)), ((), ())), preferred_element_type=F32)


def nt(a, b):
    return lax.dot_general(a, b, (((1,), (1,)), ((), ())), preferred_element_type=F32)


def tn(a, b):
    return lax.dot_general(a, b, (((0,), (0,)), ((), ())), preferred_element_type=F32)


def inv_root(values):
    return lax.rsqrt(jnp.mean(values * values, axis=-1, keepdims=True) + EPSILON)


def swap(v, axis):
    return lax.ppermute(v, axis, [(0, 1), (1, 0)])


def to_y(v, d):
    n = lax.axis_size("y")
    return lax.ppermute(v, "y", [(i, (i + d) % n) for i in range(n)])


def from_y(v, d):
    n = lax.axis_size("y")
    return lax.ppermute(v, "y", [((i + d) % n, i) for i in range(n)])


def to_plane(v, dy, dx):
    n = lax.axis_size("y")
    if dy == 0:
        return swap(v, "x")
    if dx == 0:
        return to_y(v, dy)
    perm = [(2 * i + k, 2 * ((i + dy) % n) + (k ^ dx)) for i in range(n) for k in range(2)]
    return lax.ppermute(v, ("y", "x"), perm)


def z_move(v, d):
    n = lax.axis_size("z")
    return lax.ppermute(v, "z", [(i, i + d) for i in range(n) if 0 <= i + d < n])


def add_low(*terms):
    total = terms[0].astype(F32)
    for term in terms[1:]:
        total = total + term.astype(F32)
    return total.astype(terms[0].dtype)


def plane_blocks(mine, other, y, x):
    n = lax.axis_size("y")
    rows = mine.shape[0] // (2 * n)
    got = swap(other, "core")
    blocks = {}
    for dy in range(n):
        for dx in range(2):
            place = (lax.rem(y + dy, n) * 2 + (x if dx == 0 else 1 - x)) * rows
            one = lax.dynamic_slice_in_dim(mine, place, rows, 0)
            two = lax.dynamic_slice_in_dim(got, place, rows, 0)
            blocks[(dy, dx)] = add_low(one, two)
    return blocks


def plane_total(blocks):
    return add_low(
        *[v if where == (0, 0) else to_plane(v, *where) for where, v in blocks.items()]
    )


def z_first(v):
    n = lax.axis_size("z")
    perm = [(0, 1), (3, 2)] if n == 4 else [(i, i ^ 1) for i in range(n)]
    return add_low(v, lax.ppermute(v, "z", perm))


def z_rest(v, z):
    n = lax.axis_size("z")
    if n == 4:
        whole = add_low(v, lax.ppermute(v, "z", [(1, 2), (2, 1)]))
        outer = lax.ppermute(whole, "z", [(1, 0), (2, 3)])
        return jnp.where((z == 0) | (z == 3), outer, whole)
    bit = 2
    while bit < n:
        v = add_low(v, lax.ppermute(v, "z", [(i, i ^ bit) for i in range(n)]))
        bit *= 2
    return v


def whole_grad(own, core):
    beside = swap(own, "core").astype(F32)
    own = own.astype(F32)
    return jnp.where(core == 0, own, beside), jnp.where(core == 0, beside, own)


class Gathered:
    def __init__(self, arrays, places):
        self.arrays = arrays
        self.places = places


def start_load(refs, places, dst, sems, ids, ny, shard, half_width):
    core, y, x = ids[1], ids[2], ids[3]
    copies = []
    for k, (which, (row0, rows, col0, cols), owner, row, column) in enumerate(places):
        if owner is not None:
            dy, dx = owner
            row = (lax.rem(y + dy, ny) * 2 + (x if dx == 0 else 1 - x)) * shard + row
            row = pl.multiple_of(row, 16)
        if column == "mine":
            column = pl.multiple_of(core * half_width, 128)
        elif column == "other":
            column = pl.multiple_of((1 - core) * half_width, 128)
        copy = pltpu.make_async_copy(
            refs[which].at[pl.ds(row0, rows), pl.ds(col0, cols)],
            dst.at[pl.ds(row, rows), pl.ds(column, cols)],
            sems.at[k],
        )
        copy.start()
        copies.append(copy)
    return copies


def gather_first(w_key, w_value, core):
    ny = lax.axis_size("y")
    rows, cols = w_key.shape
    h = rows // 2
    own = jnp.where(core == 0, w_key, w_value)
    from_x = swap(own, "x")
    pieces, where = [from_x], [((0, 1), 0)]
    sides = [from_y(own, d) for d in range(1, ny)]
    for d, side in enumerate(sides, 1):
        pieces.append(side)
        where.append(((d, 0), 0))
    for d, side in enumerate(sides, 1):
        pieces += [from_y(from_x[:h], d), swap(side[h:], "x")]
        where += [((d, 1), 0), ((d, 1), h)]
    mine = jnp.concatenate(pieces, axis=0)
    other = swap(mine, "core")
    places = [
        (0, (0, rows, 0, cols), (0, 0), 0, 0),
        (1, (0, rows, 0, cols), (0, 0), 0, cols),
    ]
    at = 0
    for piece, (owner, row) in zip(pieces, where):
        count = piece.shape[0]
        places.append((2, (at, count, 0, cols), owner, row, "mine"))
        places.append((3, (at, count, 0, cols), owner, row, "other"))
        at += count
    return Gathered([w_key, w_value, mine, other], places)


def gather_rest(w_query, w_out, core):
    ny = lax.axis_size("y")
    rows, cols = w_query.shape
    n = cols // 2
    half = jnp.concatenate(
        [lax.dynamic_slice(w, (0, core * n), (rows, n)) for w in (w_query, w_out)], axis=1
    )
    gathered = lax.all_gather(half, ("core", "y", "x"), axis=0, tiled=True)
    weights = []
    for k in range(2):
        places = [
            (0, ((c * 2 * ny + w) * rows, rows, k * n, n), None, w * rows, c * n)
            for c in range(2)
            for w in range(2 * ny)
        ]
        weights.append(Gathered([gathered], places))
    return weights


def gathered_matmul(lhs, weight, ids, ny, shard, width):
    count, moves = len(weight.arrays), len(weight.places)
    depth = 2 * ny * shard

    def kernel(ids_ref, lhs_ref, *refs):
        pieces, out_ref, held, sems = refs[:count], refs[count], refs[count + 1], refs[count + 2]
        for copy in start_load(pieces, weight.places, held, sems, ids_ref, ny, shard, width // 2):
            copy.wait()
        out_ref[...] = nn(lhs_ref[...], held[...]).astype(BF)

    return pl.pallas_call(
        kernel,
        out_shape=shape((lhs.shape[0], width), BF),
        in_specs=[SMEM, VMEM] + [ANY] * count,
        out_specs=VMEM,
        scratch_shapes=[pltpu.VMEM((depth, width), BF), pltpu.SemaphoreType.DMA((moves,))],
        compiler_params=params(),
        cost_estimate=cost(2 * lhs.shape[0] * depth * width, 2 * depth * width + 2 * lhs.size),
        name="project",
    )(ids, lhs, *weight.arrays)


def load_keys(nz, half, ids, refs, kv, sems):
    z = ids[0]
    slot = 2 * half

    def place(index, second):
        return kv.at[pl.ds(pl.multiple_of(index * slot + second * half, half), half)]

    copies = []
    for second in range(2):
        own, came = refs[second], refs[2 + second]
        copies.append(pltpu.make_async_copy(own.at[pl.ds(0, half)], place(0, second), sems.at[second, 0]))
        copies.append(
            pltpu.make_async_copy(own.at[pl.ds(half, half)], place(z + 1, second), sems.at[second, nz])
        )
        for d in range(1, nz):
            index = jnp.where(d <= z, d, z + 1 + nz - d)
            copies.append(
                pltpu.make_async_copy(came.at[d - 1], place(index, second), sems.at[second, d])
            )
    for copy in copies:
        copy.start()
    return copies


def slot_range(nz, ids, tile):
    z, core = ids[0], ids[1]
    if tile == 0:
        return 0, z + 1
    last = (z == nz - 1) & (core == 1)
    return jnp.where(last, 0, z + 1), nz + 1


def fill_masks(nz, half, ids, seg_col, seg_row, masks):
    z, core = ids[0], ids[1]
    blocks = 4 * nz
    own = 2 * z + core
    for tile in range(2):
        query_block = own if tile == 0 else blocks - 1 - own
        query_at = pl.multiple_of(query_block * half, half)
        query_seg = seg_row[:, pl.ds(query_at, half)]
        query_pos = query_at + lax.broadcasted_iota(jnp.int32, (1, half), 1)
        first, end = slot_range(nz, ids, tile)

        def fill(index, unused):
            for second in range(2):
                side = core if second == 0 else 1 - core
                key_block = jnp.where(
                    index <= z, 2 * (z - index) + side, blocks - 1 - (2 * (index - 1) + side)
                )
                key_at = pl.multiple_of(key_block * half, half)
                key_seg = seg_col[pl.ds(key_at, half), :]
                key_pos = key_at + lax.broadcasted_iota(jnp.int32, (half, 1), 0)
                allowed = (key_seg == query_seg) & (key_pos <= query_pos)
                masks[tile, index, second * half : (second + 1) * half, :] = jnp.where(
                    allowed, 0.0, NEG_LARGE
                )
            return unused

        lax.fori_loop(first, end, fill, 0)


def split_heads(tile_rows, scale=None):
    half = tile_rows.shape[0]
    if scale is not None:
        tile_rows = tile_rows * jnp.asarray(scale, tile_rows.dtype)
    lane = lax.broadcasted_iota(jnp.int32, (half, 128), 1)
    zero = jnp.zeros((half, 128), tile_rows.dtype)
    t0, t1, t2 = (tile_rows[:, 128 * k : 128 * k + 128] for k in range(3))

    def low(t):
        return jnp.where(lane < 64, t, zero)

    def high(t):
        return jnp.where(lane >= 64, t, zero)

    straight = jnp.concatenate([low(t0), low(t1), high(t1), high(t2)], axis=0)
    crossed = jnp.concatenate([high(t0), low(t2)], axis=0)
    return straight, crossed


def join_heads(straight_t, crossed_t, half):
    def head(t, k, upper):
        return t[64 * upper : 64 * upper + 64, half * k : half * k + half]

    tiles = (
        (head(straight_t, 0, 0), head(crossed_t, 0, 1)),
        (head(straight_t, 1, 0), head(straight_t, 2, 1)),
        (head(crossed_t, 1, 0), head(straight_t, 3, 1)),
    )
    return jnp.concatenate([jnp.concatenate(t, axis=0).T for t in tiles], axis=1)


def cross(v):
    return jnp.concatenate([v[:, 64:], v[:, :64]], axis=1)


def attention_forward(q, keys, seg_col, seg_row, ids, nz):
    rows = q.shape[0]
    half = rows // 2
    slots = nz + 1
    count = len(keys)
    slot = 2 * half
    lanes = 6 * half

    def kernel(ids_ref, q_ref, col_ref, row_ref, *refs):
        key_refs = refs[:count]
        out_ref, lse_ref, kv, scores, masks, sems = refs[count:]
        copies = load_keys(nz, half, ids_ref, key_refs, kv, sems)
        fill_masks(nz, half, ids_ref, col_ref, row_ref, masks)
        for copy in copies:
            copy.wait()
        for tile in range(2):
            first, end = slot_range(nz, ids_ref, tile)
            for pair in range(PAIRS):
                straight, crossed = split_heads(
                    q_ref[tile * half : (tile + 1) * half, 384 * pair : 384 * pair + 384], SCALE
                )

                def score(index, peak):
                    at = pl.ds(pl.multiple_of(index * slot, slot), slot)
                    k = kv[at, 128 * pair : 128 * pair + 128]
                    mask = masks[tile, index]
                    s = jnp.concatenate([nt(k, straight), nt(cross(k), crossed)], axis=1)
                    s = s + jnp.concatenate([mask] * 6, axis=1)
                    scores[index] = s
                    return jnp.maximum(peak, jnp.max(s, axis=0, keepdims=True))

                peak = lax.fori_loop(
                    first, end, score, jnp.full((1, lanes), NEG_LARGE, F32)
                )

                def mix(index, carry):
                    mass, out_s, out_c = carry
                    at = pl.ds(pl.multiple_of(index * slot, slot), slot)
                    v = kv[at, 512 + 128 * pair : 512 + 128 * pair + 128]
                    p = jnp.exp(scores[index] - peak)
                    mass = mass + jnp.sum(p, axis=0, keepdims=True)
                    p = p.astype(BF)
                    v_t = v.T
                    out_s = out_s + nn(v_t, p[:, : 4 * half])
                    out_c = out_c + nn(
                        jnp.concatenate([v_t[64:], v_t[:64]], axis=0), p[:, 4 * half :]
                    )
                    return mass, out_s, out_c

                mass, out_s, out_c = lax.fori_loop(
                    first,
                    end,
                    mix,
                    (
                        jnp.zeros((1, lanes), F32),
                        jnp.zeros((128, 4 * half), F32),
                        jnp.zeros((128, 2 * half), F32),
                    ),
                )
                share = 1.0 / mass
                out_s = out_s * share[:, : 4 * half]
                out_c = out_c * share[:, 4 * half :]
                out_ref[tile * half : (tile + 1) * half, 384 * pair : 384 * pair + 384] = (
                    join_heads(out_s, out_c, half).astype(BF)
                )
                spot = tile * PAIRS + pair
                lse_ref[spot : spot + 1, :] = peak + jnp.log(mass)

    pairs = slots * slot * half * HEADS
    return pl.pallas_call(
        kernel,
        out_shape=(shape(q.shape, BF), shape((2 * PAIRS, lanes), F32)),
        in_specs=[SMEM, VMEM, VMEM, VMEM] + [ANY] * count,
        out_specs=(VMEM, VMEM),
        scratch_shapes=[
            pltpu.VMEM((slots * slot, 1024), BF),
            pltpu.VMEM((slots, slot, lanes), F32),
            pltpu.VMEM((2, slots, slot, half), F32),
            pltpu.SemaphoreType.DMA((2, nz + 1)),
        ],
        compiler_params=params(),
        cost_estimate=cost(8 * 256 * pairs, 2 * slots * slot * 1024, pairs),
        name="attend",
    )(ids, q, seg_col, seg_row, *keys)


def attention_backward(q, keys, seg_col, seg_row, attended, grad_att, lse, ids, nz, after=()):
    rows = q.shape[0]
    half = rows // 2
    slots = nz + 1
    count = len(keys)
    slot = 2 * half
    lanes = 6 * half

    def kernel(ids_ref, q_ref, col_ref, row_ref, att_ref, grad_ref, lse_ref, *refs):
        key_refs = refs[:count]
        dq_ref, mine_ref, other_ref, kv, dkv, masks, sems = refs[count + len(after) :]
        copies = load_keys(nz, half, ids_ref, key_refs, kv, sems)
        fill_masks(nz, half, ids_ref, col_ref, row_ref, masks)
        dkv[...] = jnp.zeros_like(dkv)
        for copy in copies:
            copy.wait()
        for tile in range(2):
            first, end = slot_range(nz, ids_ref, tile)
            for pair in range(PAIRS):
                here = (slice(tile * half, (tile + 1) * half), slice(384 * pair, 384 * pair + 384))
                q_s, q_c = split_heads(q_ref[here], SCALE)
                g_s, g_c = split_heads(grad_ref[here])
                product = grad_ref[here].astype(F32) * att_ref[here].astype(F32)
                turned = [product[:, 128 * k : 128 * k + 128].T for k in range(3)]
                lower = [jnp.sum(t[:64], axis=0, keepdims=True) for t in turned]
                upper = [jnp.sum(t[64:], axis=0, keepdims=True) for t in turned]
                delta = jnp.concatenate(
                    [lower[0], lower[1], upper[1], upper[2], upper[0], lower[2]], axis=1
                )
                spot = tile * PAIRS + pair
                total = lse_ref[spot : spot + 1, :]

                def step(index, carry):
                    dq_s, dq_c = carry
                    at = pl.ds(pl.multiple_of(index * slot, slot), slot)
                    k_lanes = slice(128 * pair, 128 * pair + 128)
                    v_lanes = slice(512 + 128 * pair, 512 + 128 * pair + 128)
                    k, v = kv[at, k_lanes], kv[at, v_lanes]
                    mask = masks[tile, index]
                    s = jnp.concatenate([nt(k, q_s), nt(cross(k), q_c)], axis=1)
                    p = jnp.exp(s + jnp.concatenate([mask] * 6, axis=1) - total)
                    dp = jnp.concatenate([nt(v, g_s), nt(cross(v), g_c)], axis=1)
                    ds = (p * (dp - delta)).astype(BF)
                    p = p.astype(BF)
                    dkv[at, v_lanes] += nn(p[:, : 4 * half], g_s) + cross(
                        nn(p[:, 4 * half :], g_c)
                    )
                    dkv[at, k_lanes] += nn(ds[:, : 4 * half], q_s) + cross(
                        nn(ds[:, 4 * half :], q_c)
                    )
                    k_t = k.T
                    dq_s = dq_s + nn(k_t, ds[:, : 4 * half])
                    dq_c = dq_c + nn(
                        jnp.concatenate([k_t[64:], k_t[:64]], axis=0), ds[:, 4 * half :]
                    )
                    return dq_s, dq_c

                dq_s, dq_c = lax.fori_loop(
                    first,
                    end,
                    step,
                    (jnp.zeros((128, 4 * half), F32), jnp.zeros((128, 2 * half), F32)),
                )
                dq_ref[here] = (SCALE * join_heads(dq_s, dq_c, half)).astype(BF)
        for index in range(slots):
            mine_ref[index] = dkv[index * slot : index * slot + half, :].astype(BF)
            other_ref[index] = dkv[index * slot + half : (index + 1) * slot, :].astype(BF)

    pairs = slots * slot * half * HEADS
    return pl.pallas_call(
        kernel,
        out_shape=(
            shape(q.shape, BF),
            shape((slots, half, 1024), BF),
            shape((slots, half, 1024), BF),
        ),
        in_specs=[SMEM] + [VMEM] * 6 + [ANY] * (count + len(after)),
        out_specs=(VMEM,) * 3,
        scratch_shapes=[
            pltpu.VMEM((slots * slot, 1024), BF),
            pltpu.VMEM((slots * slot, 1024), F32),
            pltpu.VMEM((2, slots, slot, half), F32),
            pltpu.SemaphoreType.DMA((2, nz + 1)),
        ],
        compiler_params=params(),
        cost_estimate=cost(300 * 256 * pairs, 2 * slots * slot * 1024, pairs),
        name="attend_back",
    )(ids, q, seg_col, seg_row, attended, grad_att, lse, *keys, *after)


def out_project(tokens, attended, gain, weight, ids, ny, shard):
    rows, width = tokens.shape
    count, moves = len(weight.arrays), len(weight.places)

    def kernel(ids_ref, tokens_ref, att_ref, gain_ref, *refs):
        pieces = refs[:count]
        resid_ref, norm_ref, held, sems = refs[count:]
        for copy in start_load(pieces, weight.places, held, sems, ids_ref, ny, shard, width // 2):
            copy.wait()
        resid = tokens_ref[...].astype(F32) + nn(att_ref[...], held[...])
        resid_ref[...] = resid
        norm_ref[...] = (resid * inv_root(resid) * gain_ref[...]).astype(BF)

    return pl.pallas_call(
        kernel,
        out_shape=(shape((rows, width), F32), shape((rows, width), BF)),
        in_specs=[SMEM] + [VMEM] * 3 + [ANY] * count,
        out_specs=(VMEM, VMEM),
        scratch_shapes=[pltpu.VMEM((width, width), BF), pltpu.SemaphoreType.DMA((moves,))],
        compiler_params=params(),
        cost_estimate=cost(2 * rows * width * width, 2 * width * width + 10 * rows * width),
        name="out_project",
    )(ids, tokens, attended, gain, *weight.arrays)


def out_back(resid, cotangent, gain, terms, weight, ids, ny, shard, after=()):
    rows, width = resid.shape
    count, moves = len(weight.arrays), len(weight.places)
    term_count = len(terms)

    def kernel(ids_ref, resid_ref, cot_ref, gain_ref, *refs):
        term_refs, pieces = refs[:term_count], refs[term_count : term_count + count]
        gres_ref, branch_ref, gatt_ref, ggain_ref, held, sems = refs[term_count + count + len(after) :]
        copies = start_load(pieces, weight.places, held, sems, ids_ref, ny, shard, width // 2)
        grad_norm = term_refs[0][...].astype(F32)
        for ref in term_refs[1:]:
            grad_norm = grad_norm + ref[...].astype(F32)
        resid = resid_ref[...]
        root = inv_root(resid)
        s = resid * root
        ggain_ref[...] = jnp.sum(grad_norm * s, axis=0, keepdims=True)
        t = grad_norm * gain_ref[...]
        gres = cot_ref[...].astype(F32) + root * (
            t - s * jnp.mean(t * s, axis=-1, keepdims=True)
        )
        gres_ref[...] = gres
        branch = gres.astype(BF)
        branch_ref[...] = branch
        for copy in copies:
            copy.wait()
        gatt_ref[...] = nt(branch, held[...]).astype(BF)

    return pl.pallas_call(
        kernel,
        out_shape=(
            shape((rows, width), F32),
            shape((rows, width), BF),
            shape((rows, width), BF),
            shape((1, width), F32),
        ),
        in_specs=[SMEM] + [VMEM] * (3 + term_count) + [ANY] * (count + len(after)),
        out_specs=(VMEM,) * 4,
        scratch_shapes=[pltpu.VMEM((width, width), BF), pltpu.SemaphoreType.DMA((moves,))],
        compiler_params=params(),
        cost_estimate=cost(2 * rows * width * width, 2 * width * width + 20 * rows * width),
        name="out_back",
    )(ids, resid, cotangent, gain, *terms, *weight.arrays, *after)


def in_back(tokens, gres, gain, dq, dkv, weight_q, weight_kv, ids, ny, shard, after=()):
    rows, width = tokens.shape
    kv_width = dkv.shape[1]
    count_q, count_kv = len(weight_q.arrays), len(weight_kv.arrays)

    def kernel(ids_ref, tokens_ref, gres_ref, gain_ref, dq_ref, dkv_ref, *refs):
        q_pieces, kv_pieces = refs[:count_q], refs[count_q : count_q + count_kv]
        out_ref, ggain_ref, held_q, held_kv, sems_q, sems_kv = refs[count_q + count_kv + len(after) :]
        copies = start_load(
            kv_pieces, weight_kv.places, held_kv, sems_kv, ids_ref, ny, shard, kv_width // 2
        ) + start_load(q_pieces, weight_q.places, held_q, sems_q, ids_ref, ny, shard, width // 2)
        for copy in copies:
            copy.wait()
        grad_norm = nt(dq_ref[...], held_q[...]) + nt(dkv_ref[...], held_kv[...])
        x = tokens_ref[...].astype(F32)
        root = inv_root(x)
        s = x * root
        ggain_ref[...] = jnp.sum(grad_norm * s, axis=0, keepdims=True)
        t = grad_norm * gain_ref[...]
        out_ref[...] = gres_ref[...] + root * (t - s * jnp.mean(t * s, axis=-1, keepdims=True))

    return pl.pallas_call(
        kernel,
        out_shape=(shape((rows, width), F32), shape((1, width), F32)),
        in_specs=[SMEM] + [VMEM] * 5 + [ANY] * (count_q + count_kv + len(after)),
        out_specs=(VMEM, VMEM),
        scratch_shapes=[
            pltpu.VMEM((width, width), BF),
            pltpu.VMEM((width, kv_width), BF),
            pltpu.SemaphoreType.DMA((len(weight_q.places),)),
            pltpu.SemaphoreType.DMA((len(weight_kv.places),)),
        ],
        compiler_params=params(),
        cost_estimate=cost(
            2 * rows * width * (width + kv_width), 2 * width * (width + kv_width) + 12 * rows * width
        ),
        name="in_back",
    )(ids, tokens, gres, gain, dq, dkv, *weight_q.arrays, *weight_kv.arrays, *after)


def expert_block(block_ids, blocks, cot_all, coeffs, w_gate, w_up, w_down, out_dtype, after=()):
    experts, width, units = w_gate.shape
    pieces = [p for block in blocks for p in block]
    count, many, extra = len(pieces), len(blocks), len(after)
    size = coeffs[0].shape[0]
    rows = many * size

    def kernel(id_ref, *refs):
        n_refs, refs = refs[:count], refs[count:]
        c_refs, refs = refs[:many], refs[many:]
        (coeff_ref, wg_ref, wu_ref, wd_ref), refs = refs[:4], refs[4 + extra :]
        (hid_ref, gg_ref, gu_ref), refs = refs[:3], refs[3:]
        mix_refs, gnf_refs, (mix, gnf) = refs[:many], refs[many : 2 * many], refs[2 * many :]
        e = pl.program_id(0)
        wg, wu, wd = wg_ref[0], wu_ref[0], wd_ref[0]
        rows_in = jnp.concatenate([ref[...] for ref in n_refs], axis=0)
        cot = jnp.concatenate([ref[...] for ref in c_refs], axis=0)
        lane = lax.broadcasted_iota(jnp.int32, coeff_ref.shape, 1)
        weight = jnp.sum(jnp.where(lane == e, coeff_ref[...], 0.0), axis=1, keepdims=True)
        gate = nn(rows_in, wg)
        up = nn(rows_in, wu)
        back = nt(cot, wd) * weight
        sigma = jax.nn.sigmoid(gate)
        silu = gate * sigma
        hidden = (silu * up * weight).astype(BF)
        grad_gate = (back * up * sigma * (1.0 + gate * (1.0 - sigma))).astype(BF)
        grad_up = (back * silu).astype(BF)
        hid_ref[...] = hidden
        gg_ref[...] = grad_gate
        gu_ref[...] = grad_up
        more = nt(grad_gate, wg) + nt(grad_up, wu)
        out = nn(hidden, wd)

        @pl.when(e == 0)
        def _():
            gnf[...] = more
            mix[...] = out

        @pl.when(e > 0)
        def _():
            gnf[...] += more
            mix[...] += out

        @pl.when(e == experts - 1)
        def _():
            for k in range(many):
                here = slice(k * size, (k + 1) * size)
                gnf_refs[k][...] = gnf[here].astype(out_dtype)
                mix_refs[k][...] = mix[here].astype(out_dtype)

    keep = pl.BlockSpec((size, width), lambda e, s: (0, 0))
    unit = pl.BlockSpec((rows, units), lambda e, s: (0, e))
    outs = pl.pallas_call(
        kernel,
        grid_spec=pltpu.PrefetchScalarGridSpec(
            num_scalar_prefetch=1,
            grid=(experts,),
            in_specs=[pl.BlockSpec(p.shape, lambda e, s: (0, 0)) for p in pieces]
            + [pl.BlockSpec((size, width), lambda e, s, k=k: (s[k], 0)) for k in range(many)]
            + [
                pl.BlockSpec((rows, experts), lambda e, s: (0, 0)),
                pl.BlockSpec((1, width, units), lambda e, s: (e, 0, 0)),
                pl.BlockSpec((1, width, units), lambda e, s: (e, 0, 0)),
                pl.BlockSpec((1, units, width), lambda e, s: (e, 0, 0)),
            ]
            + [ANY] * extra,
            out_specs=(unit,) * 3 + (keep,) * (2 * many),
            scratch_shapes=[pltpu.VMEM((rows, width), F32)] * 2,
        ),
        out_shape=(shape((rows, experts * units), BF),) * 3
        + (shape((size, width), out_dtype),) * (2 * many),
        compiler_params=params(),
        cost_estimate=cost(
            12 * rows * width * experts * units, 6 * experts * width * units + 10 * rows * width
        ),
        name="experts",
    )(
        block_ids,
        *pieces,
        *[cot_all] * many,
        jnp.concatenate(coeffs, axis=0),
        w_gate,
        w_up,
        w_down,
        *after,
    )
    return outs[:3], outs[3 : 3 + many], outs[3 + many :]


def expert_grads(block_ids, pieces, cot_all, hidden, grad_gate, grad_up, experts, size):
    groups = len(hidden)
    width = cot_all.shape[1]
    units = hidden[0].shape[1] // experts
    count = len(pieces)
    blocks = block_ids.shape[0]
    rows = blocks * size

    def kernel(id_ref, *refs):
        n_refs, c_ref = refs[:count], refs[count]
        at = count + 1
        h_refs, gg_refs, gu_refs = (
            refs[at : at + groups],
            refs[at + groups : at + 2 * groups],
            refs[at + 2 * groups : at + 3 * groups],
        )
        out_ref, n_all, c_all, n_sems, c_sems = refs[at + 3 * groups :]

        @pl.when(pl.program_id(0) == 0)
        def _():
            copies, row = [], 0
            for k, ref in enumerate(n_refs):
                copies.append(
                    pltpu.make_async_copy(ref, n_all.at[pl.ds(row, ref.shape[0])], n_sems.at[k])
                )
                row += ref.shape[0]
            for k in range(blocks):
                start = pl.multiple_of(id_ref[k] * size, size)
                copies.append(
                    pltpu.make_async_copy(
                        c_ref.at[pl.ds(start, size)], c_all.at[pl.ds(k * size, size)], c_sems.at[k]
                    )
                )
            for copy in copies:
                copy.start()
            for copy in copies:
                copy.wait()

        grads = jnp.concatenate(
            [
                jnp.concatenate([ref[...] for ref in gg_refs], axis=0),
                jnp.concatenate([ref[...] for ref in gu_refs], axis=0),
            ],
            axis=1,
        )
        out_ref[:, : 2 * units] = tn(n_all[...], grads).astype(BF)
        hid = jnp.concatenate([ref[...] for ref in h_refs], axis=0)
        out_ref[:, 2 * units :] = tn(c_all[...], hid).astype(BF)

    grid_spec = pltpu.PrefetchScalarGridSpec(
        num_scalar_prefetch=1,
        grid=(experts,),
        in_specs=[ANY] * (count + 1)
        + [
            pl.BlockSpec((one.shape[0], units), lambda e, s: (0, e))
            for group in (hidden, grad_gate, grad_up)
            for one in group
        ],
        out_specs=pl.BlockSpec((width, 3 * units), lambda e, s: (e, 0)),
        scratch_shapes=[
            pltpu.VMEM((rows, width), BF),
            pltpu.VMEM((rows, width), BF),
            pltpu.SemaphoreType.DMA((count,)),
            pltpu.SemaphoreType.DMA((blocks,)),
        ],
    )
    return pl.pallas_call(
        kernel,
        grid_spec=grid_spec,
        out_shape=shape((experts * width, 3 * units), BF),
        compiler_params=params(),
        cost_estimate=cost(
            6 * rows * width * units * experts, 4 * rows * width + 6 * experts * units * width
        ),
        name="expert_grads",
    )(block_ids, *pieces, cot_all, *hidden, *grad_gate, *grad_up)


def spread_grads(grads, experts):
    width, units = grads.shape[0] // experts, grads.shape[1] // 3

    def kernel(in_ref, gate_ref, up_ref, down_ref):
        gate_ref[0] = in_ref[:, :units].astype(F32)
        up_ref[0] = in_ref[:, units : 2 * units].astype(F32)
        down_ref[0] = in_ref[:, 2 * units :].astype(F32).T

    side = pl.BlockSpec((1, width, units), lambda e: (e, 0, 0))
    return pl.pallas_call(
        kernel,
        grid=(experts,),
        out_shape=(shape((experts, width, units), F32),) * 2
        + (shape((experts, units, width), F32),),
        in_specs=[pl.BlockSpec((width, 3 * units), lambda e: (e, 0))],
        out_specs=(side, side, pl.BlockSpec((1, units, width), lambda e: (e, 0, 0))),
        compiler_params=params(),
        cost_estimate=cost(0, 6 * grads.size),
        name="spread_grads",
    )(grads)


def tie(values, *after):
    return pl.pallas_call(
        lambda *refs: None,
        out_shape=[shape(v.shape, v.dtype) for v in values],
        in_specs=[ANY] * (len(values) + len(after)),
        out_specs=[ANY] * len(values),
        input_output_aliases={k: k for k in range(len(values))},
        compiler_params=params(),
        cost_estimate=cost(0, 0),
        name="tie",
    )(*values, *after)


def weight_grads(ids, pairs, extra=(), after=()):
    depth = pairs[0][0].shape[1]
    halves = [right.shape[1] // 2 for _, right in pairs]
    width = sum(halves) + (128 if extra else 0)
    rows = pairs[0][0].shape[0]
    inputs = 2 * len(pairs) + len(extra)

    def kernel(ids_ref, *refs):
        mine_ref, other_ref = refs[inputs + len(after) :]
        core, at = ids_ref[1], 0
        for k, n in enumerate(halves):
            left, right = refs[2 * k][...], refs[2 * k + 1]
            for out_ref, side in ((mine_ref, core), (other_ref, 1 - core)):
                columns = right[:, pl.ds(pl.multiple_of(side * n, 128), n)]
                out_ref[:, at : at + n] = tn(left, columns).astype(BF)
            at += n
        if extra:
            lines = [ref[...] for ref in refs[2 * len(pairs) : inputs]]
            lines.append(jnp.zeros((128 - len(extra), depth), F32))
            turned = jnp.concatenate(lines, axis=0).T.astype(BF)
            mine_ref[:, at:] = turned
            other_ref[:, at:] = turned

    return pl.pallas_call(
        kernel,
        out_shape=(shape((depth, width), BF),) * 2,
        in_specs=[SMEM] + [VMEM] * inputs + [ANY] * len(after),
        out_specs=(VMEM,) * 2,
        compiler_params=params(),
        cost_estimate=cost(4 * rows * depth * width, 4 * depth * width),
        name="weight_grads",
    )(ids, *[v for pair in pairs for v in pair], *extra, *after)


def body(
    tokens,
    segments,
    routes,
    route_weights,
    gain_attn,
    w_query,
    w_key,
    w_value,
    w_out,
    gain_ffn,
    w_gate,
    w_up,
    w_down,
    cotangent,
):
    tokens, cotangent = tokens[0], cotangent[0]
    rows, width = tokens.shape
    half = rows // 2
    nz, ny = lax.axis_size("z"), lax.axis_size("y")
    z, core, y, x = (lax.axis_index(a) for a in ("z", "core", "y", "x"))
    ids = jnp.stack([z, core, y, x]).astype(jnp.int32)
    shard = w_query.shape[0]
    experts = w_gate.shape[0]
    kv_width = w_key.shape[1] + w_value.shape[1]
    plane = [(dy, dx) for dy in range(ny) for dx in range(2)]
    seg_row = segments
    seg_col = segments.reshape(-1, 1)

    chosen = routes[0][:, :, None] == jnp.arange(experts, dtype=jnp.int32)[None, None, :]
    coeff = jnp.sum(jnp.where(chosen, route_weights[0][:, :, None], 0.0), axis=1)
    small = jnp.concatenate(
        [coeff.reshape(-1), gain_attn.astype(F32), gain_ffn.astype(F32)]
    ).reshape(-1, 128)
    coeffs = {}
    slot = jnp.arange(2 * ny, dtype=jnp.int32)[None, :, None]
    gains = jnp.zeros((2, 2 * ny, shard), F32)
    owners = {}
    for dy, dx in plane:
        got = small if (dy, dx) == (0, 0) else to_plane(small, -dy % ny, dx)
        got = got.reshape(-1)
        owner = lax.rem(y + dy, ny) * 2 + (x if dx == 0 else 1 - x)
        owners[(dy, dx)] = owner.astype(jnp.int32).reshape(1)
        coeffs[(dy, dx)] = got[: rows * experts].reshape(rows, experts)
        pair = got[rows * experts :].reshape(2, 1, shard)
        gains = gains + jnp.where(slot == owner, pair, 0.0)
    gain_a, gain_f = gains[0].reshape(1, width), gains[1].reshape(1, width)

    weight_kv = gather_first(w_key, w_value, core)
    weight_q, weight_o = gather_rest(w_query, w_out, core)
    cot_all = lax.all_gather(cotangent, ("y", "x"), axis=0, tiled=True)

    x_f = tokens.astype(F32)
    normed = (x_f * inv_root(x_f) * gain_a).astype(BF)
    kv = gathered_matmul(normed, weight_kv, ids, ny, shard, kv_width)
    beside = swap(kv, "core")
    came = []
    for d in range(1, nz):
        start = jnp.where(z + d < nz, 0, half)
        piece = lax.dynamic_slice_in_dim(kv, start, half, 0)
        came.append(lax.ppermute(piece, "z", [(i, (i + d) % nz) for i in range(nz)]))
    came = jnp.stack(came)
    keys = [kv, beside, came, swap(came, "core")]
    queries = gathered_matmul(normed, weight_q, ids, ny, shard, width)
    attended, lse = attention_forward(queries, keys, seg_col, seg_row, ids, nz)
    resid, normed_f = out_project(tokens, attended, gain_f, weight_o, ids, ny, shard)

    from_x = swap(normed_f, "x")
    norms = {(0, 0): [normed_f], (0, 1): [from_x]}
    for d in range(1, ny):
        side = from_y(normed_f, d)
        norms[(d, 0)] = [side]
        norms[(d, 1)] = [from_y(from_x[:half], d), swap(side[half:], "x")]
    groups = [
        [(0, 0)],
        [(0, 1)] + [(d, 0) for d in range(1, ny)],
        [(d, 1) for d in range(1, ny)],
    ]
    hidden, grad_gate, grad_up, mixes, grad_norms, after = [], [], [], [], [], ()
    for group in groups:
        own = group == [(0, 0)]
        (h, gg, gu), mix, gnf = expert_block(
            jnp.concatenate([jnp.zeros_like(owners[where]) if own else owners[where] for where in group]),
            [norms[where] for where in group],
            cotangent if own else cot_all,
            [coeffs[where] for where in group],
            w_gate,
            w_up,
            w_down,
            F32 if own else BF,
            after,
        )
        after = (h,)
        hidden.append(h)
        grad_gate.append(gg)
        grad_up.append(gu)
        for where, one, two in zip(group, mix, gnf):
            mixes.append(one)
            grad_norms.append(two if own else to_plane(two, *where))
    order = [where for group in groups for where in group]
    expert_parts = expert_grads(
        jnp.concatenate([owners[where] for where in order]),
        [piece for where in order for piece in norms[where]],
        cot_all,
        hidden,
        grad_gate,
        grad_up,
        experts,
        rows,
    )
    expert_shard = lax.psum_scatter(
        expert_parts, ("z", "core"), scatter_dimension=0, tiled=True
    )
    gres, branch, grad_att, ggain_f = out_back(
        resid, cotangent, gain_f, grad_norms, weight_o, ids, ny, shard, (expert_parts,)
    )
    mixes[1:] = tie(mixes[1:], branch)
    result, came = resid, []
    for where, mix in zip(order, mixes):
        mix = mix if where == (0, 0) else to_plane(mix, *where)
        came.append(mix)
        result = result + mix.astype(F32)
    result = result.astype(BF)
    o_grads = weight_grads(ids, [(attended, branch)])
    dq, dkv_mine, dkv_other = attention_backward(
        queries, keys, seg_col, seg_row, attended, grad_att, lse, ids, nz, o_grads[:1]
    )
    q_grads = weight_grads(ids, [(normed, dq)], (), came[1:])
    parts = add_low(dkv_mine, swap(dkv_other, "core"))
    low = parts[0].astype(F32)
    high = lax.dynamic_index_in_dim(parts, z + 1, 0, keepdims=False).astype(F32)
    for d in range(1, nz):
        index = jnp.where(d <= z, d, z + 1 + nz - d)
        piece = lax.dynamic_index_in_dim(parts, index, 0, keepdims=False)
        got = lax.ppermute(piece, "z", [((i + d) % nz, i) for i in range(nz)]).astype(F32)
        low = low + jnp.where(z + d < nz, got, 0.0)
        high = high + jnp.where(z + d < nz, 0.0, got)
    dkv = jnp.concatenate([low, high], axis=0).astype(BF)
    o_blocks, q_blocks = plane_blocks(*o_grads, y, x), plane_blocks(*q_grads, y, x)
    o_total, q_total = plane_total(o_blocks), plane_total(q_blocks)
    (expert_shard,) = tie([expert_shard], o_total, q_total, dkv)
    expert_totals = spread_grads(
        lax.all_gather(expert_shard, ("z", "core"), axis=0, tiled=True), experts
    )
    grad_tokens, ggain_a = in_back(
        tokens, gres, gain_a, dq, dkv, weight_q, weight_kv, ids, ny, shard
    )
    o_first, q_first = z_first(o_total), z_first(q_total)
    kv_grads = weight_grads(ids, [(normed, dkv)], (ggain_a, ggain_f), (o_first,))
    kv_blocks = plane_blocks(*kv_grads, y, x)
    grad_wo = jnp.concatenate(whole_grad(z_rest(o_first, z), core), axis=1)
    grad_wq = jnp.concatenate(whole_grad(z_rest(q_first, z), core), axis=1)
    kv_first = z_first(plane_total(kv_blocks))
    grad_wk, grad_wv = whole_grad(z_rest(kv_first, z), core)
    ggain_a, ggain_f = grad_wk[:, -128], grad_wk[:, -127]
    grad_wk, grad_wv = grad_wk[:, :-128], grad_wv[:, :-128]
    return (
        result[None],
        grad_tokens[None],
        ggain_a,
        grad_wq,
        grad_wk,
        grad_wv,
        grad_wo,
        ggain_f,
        *expert_totals,
    )


def solution(mesh):
    ctx, wt = mesh.shape["ctx"], mesh.shape["wt"]
    fine = Mesh(mesh.devices.reshape(ctx // 2, 2, wt // 2, 2), ("z", "core", "y", "x"))
    c, w = ("z", "core"), ("y", "x")
    rows = P(w, c, None)
    return jax.shard_map(
        body,
        mesh=fine,
        in_specs=(
            rows,
            P(w, None),
            rows,
            rows,
            P(w),
            P(w, None),
            P(w, None),
            P(w, None),
            P(w, None),
            P(w),
            P(None, None, w),
            P(None, None, w),
            P(None, w, None),
            rows,
        ),
        out_specs=(
            rows,
            rows,
            P(w),
            P(w, None),
            P(w, None),
            P(w, None),
            P(w, None),
            P(w),
            P(None, None, w),
            P(None, None, w),
            P(None, w, None),
        ),
        check_vma=False,
    )
```

```python
import jax
import jax.numpy as jnp
from jax import lax
from jax.experimental import pallas as pl
from jax.experimental.pallas import tpu as pltpu
from jax.sharding import Mesh, PartitionSpec as P

HEADS = 24
KV_HEADS = 8
HEAD_DIM = 64
SCALE = HEAD_DIM ** -0.5
PAIRS = KV_HEADS // 2
EPSILON = 1e-06
NEG_LARGE = -1e30
VMEM_BYTES = 56 * 1024 * 1024
BF = jnp.bfloat16
F32 = jnp.float32

VMEM = pl.BlockSpec(memory_space=pltpu.VMEM)
SMEM = pl.BlockSpec(memory_space=pltpu.SMEM)
ANY = pl.BlockSpec(memory_space=pl.ANY)


def params():
    return pltpu.CompilerParams(vmem_limit_bytes=VMEM_BYTES)


def cost(flops, nbytes, trans=0):
    return pl.CostEstimate(flops=int(flops), bytes_accessed=int(nbytes), transcendentals=int(trans))


def shape(dims, dtype):
    return jax.ShapeDtypeStruct(tuple(dims), dtype)


def nn(a, b):
    return lax.dot_general(a, b, (((1,), (0,)), ((), ())), preferred_element_type=F32)


def nt(a, b):
    return lax.dot_general(a, b, (((1,), (1,)), ((), ())), preferred_element_type=F32)


def tn(a, b):
    return lax.dot_general(a, b, (((0,), (0,)), ((), ())), preferred_element_type=F32)


def inv_root(values):
    return lax.rsqrt(jnp.mean(values * values, axis=-1, keepdims=True) + EPSILON)


def swap(v, axis):
    return lax.ppermute(v, axis, [(0, 1), (1, 0)])


def to_y(v, d):
    n = lax.axis_size("y")
    return lax.ppermute(v, "y", [(i, (i + d) % n) for i in range(n)])


def from_y(v, d):
    n = lax.axis_size("y")
    return lax.ppermute(v, "y", [((i + d) % n, i) for i in range(n)])


def to_plane(v, dy, dx):
    n = lax.axis_size("y")
    if dy == 0:
        return swap(v, "x")
    if dx == 0:
        return to_y(v, dy)
    perm = [(2 * i + k, 2 * ((i + dy) % n) + (k ^ dx)) for i in range(n) for k in range(2)]
    return lax.ppermute(v, ("y", "x"), perm)


def z_move(v, d):
    n = lax.axis_size("z")
    return lax.ppermute(v, "z", [(i, i + d) for i in range(n) if 0 <= i + d < n])


def add_low(*terms):
    total = terms[0].astype(F32)
    for term in terms[1:]:
        total = total + term.astype(F32)
    return total.astype(terms[0].dtype)


def plane_blocks(mine, other, y, x):
    n = lax.axis_size("y")
    rows = mine.shape[0] // (2 * n)
    got = swap(other, "core")
    blocks = {}
    for dy in range(n):
        for dx in range(2):
            place = (lax.rem(y + dy, n) * 2 + (x if dx == 0 else 1 - x)) * rows
            one = lax.dynamic_slice_in_dim(mine, place, rows, 0)
            two = lax.dynamic_slice_in_dim(got, place, rows, 0)
            blocks[(dy, dx)] = add_low(one, two)
    return blocks


def plane_total(blocks):
    return add_low(
        *[v if where == (0, 0) else to_plane(v, *where) for where, v in blocks.items()]
    )


def z_first(v):
    n = lax.axis_size("z")
    perm = [(0, 1), (3, 2)] if n == 4 else [(i, i ^ 1) for i in range(n)]
    return add_low(v, lax.ppermute(v, "z", perm))


def z_rest(v, z):
    n = lax.axis_size("z")
    if n == 4:
        whole = add_low(v, lax.ppermute(v, "z", [(1, 2), (2, 1)]))
        outer = lax.ppermute(whole, "z", [(1, 0), (2, 3)])
        return jnp.where((z == 0) | (z == 3), outer, whole)
    bit = 2
    while bit < n:
        v = add_low(v, lax.ppermute(v, "z", [(i, i ^ bit) for i in range(n)]))
        bit *= 2
    return v


def whole_grad(own, core):
    beside = swap(own, "core").astype(F32)
    own = own.astype(F32)
    return jnp.where(core == 0, own, beside), jnp.where(core == 0, beside, own)


class Gathered:
    def __init__(self, arrays, places):
        self.arrays = arrays
        self.places = places


def start_load(refs, places, dst, sems, ids, ny, shard, half_width):
    core, y, x = ids[1], ids[2], ids[3]
    copies = []
    for k, (which, (row0, rows, col0, cols), owner, row, column) in enumerate(places):
        if owner is not None:
            dy, dx = owner
            row = (lax.rem(y + dy, ny) * 2 + (x if dx == 0 else 1 - x)) * shard + row
            row = pl.multiple_of(row, 16)
        if column == "mine":
            column = pl.multiple_of(core * half_width, 128)
        elif column == "other":
            column = pl.multiple_of((1 - core) * half_width, 128)
        copy = pltpu.make_async_copy(
            refs[which].at[pl.ds(row0, rows), pl.ds(col0, cols)],
            dst.at[pl.ds(row, rows), pl.ds(column, cols)],
            sems.at[k],
        )
        copy.start()
        copies.append(copy)
    return copies


def gather_first(w_key, w_value, core):
    ny = lax.axis_size("y")
    rows, cols = w_key.shape
    h = rows // 2
    own = jnp.where(core == 0, w_key, w_value)
    from_x = swap(own, "x")
    pieces, where = [from_x], [((0, 1), 0)]
    sides = [from_y(own, d) for d in range(1, ny)]
    for d, side in enumerate(sides, 1):
        pieces.append(side)
        where.append(((d, 0), 0))
    for d, side in enumerate(sides, 1):
        pieces += [from_y(from_x[:h], d), swap(side[h:], "x")]
        where += [((d, 1), 0), ((d, 1), h)]
    mine = jnp.concatenate(pieces, axis=0)
    other = swap(mine, "core")
    places = [
        (0, (0, rows, 0, cols), (0, 0), 0, 0),
        (1, (0, rows, 0, cols), (0, 0), 0, cols),
    ]
    at = 0
    for piece, (owner, row) in zip(pieces, where):
        count = piece.shape[0]
        places.append((2, (at, count, 0, cols), owner, row, "mine"))
        places.append((3, (at, count, 0, cols), owner, row, "other"))
        at += count
    return Gathered([w_key, w_value, mine, other], places)


def gather_rest(w_query, w_out, core):
    ny = lax.axis_size("y")
    rows, cols = w_query.shape
    n = cols // 2
    half = jnp.concatenate(
        [lax.dynamic_slice(w, (0, core * n), (rows, n)) for w in (w_query, w_out)], axis=1
    )
    gathered = lax.all_gather(half, ("core", "y", "x"), axis=0, tiled=True)
    weights = []
    for k in range(2):
        places = [
            (0, ((c * 2 * ny + w) * rows, rows, k * n, n), None, w * rows, c * n)
            for c in range(2)
            for w in range(2 * ny)
        ]
        weights.append(Gathered([gathered], places))
    return weights


def gathered_matmul(lhs, weight, ids, ny, shard, width):
    count, moves = len(weight.arrays), len(weight.places)
    depth = 2 * ny * shard

    def kernel(ids_ref, lhs_ref, *refs):
        pieces, out_ref, held, sems = refs[:count], refs[count], refs[count + 1], refs[count + 2]
        for copy in start_load(pieces, weight.places, held, sems, ids_ref, ny, shard, width // 2):
            copy.wait()
        out_ref[...] = nn(lhs_ref[...], held[...]).astype(BF)

    return pl.pallas_call(
        kernel,
        out_shape=shape((lhs.shape[0], width), BF),
        in_specs=[SMEM, VMEM] + [ANY] * count,
        out_specs=VMEM,
        scratch_shapes=[pltpu.VMEM((depth, width), BF), pltpu.SemaphoreType.DMA((moves,))],
        compiler_params=params(),
        cost_estimate=cost(2 * lhs.shape[0] * depth * width, 2 * depth * width + 2 * lhs.size),
        name="project",
    )(ids, lhs, *weight.arrays)


def load_keys(nz, half, ids, refs, kv, sems):
    z = ids[0]
    slot = 2 * half

    def place(index, second):
        return kv.at[pl.ds(pl.multiple_of(index * slot + second * half, half), half)]

    copies = []
    for second in range(2):
        own, came = refs[second], refs[2 + second]
        copies.append(pltpu.make_async_copy(own.at[pl.ds(0, half)], place(0, second), sems.at[second, 0]))
        copies.append(
            pltpu.make_async_copy(own.at[pl.ds(half, half)], place(z + 1, second), sems.at[second, nz])
        )
        for d in range(1, nz):
            index = jnp.where(d <= z, d, z + 1 + nz - d)
            copies.append(
                pltpu.make_async_copy(came.at[d - 1], place(index, second), sems.at[second, d])
            )
    for copy in copies:
        copy.start()
    return copies


def slot_range(nz, ids, tile):
    z, core = ids[0], ids[1]
    if tile == 0:
        return 0, z + 1
    last = (z == nz - 1) & (core == 1)
    return jnp.where(last, 0, z + 1), nz + 1


def fill_masks(nz, half, ids, seg_col, seg_row, masks):
    z, core = ids[0], ids[1]
    blocks = 4 * nz
    own = 2 * z + core
    for tile in range(2):
        query_block = own if tile == 0 else blocks - 1 - own
        query_at = pl.multiple_of(query_block * half, half)
        query_seg = seg_row[:, pl.ds(query_at, half)]
        query_pos = query_at + lax.broadcasted_iota(jnp.int32, (1, half), 1)
        first, end = slot_range(nz, ids, tile)

        def fill(index, unused):
            for second in range(2):
                side = core if second == 0 else 1 - core
                key_block = jnp.where(
                    index <= z, 2 * (z - index) + side, blocks - 1 - (2 * (index - 1) + side)
                )
                key_at = pl.multiple_of(key_block * half, half)
                key_seg = seg_col[pl.ds(key_at, half), :]
                key_pos = key_at + lax.broadcasted_iota(jnp.int32, (half, 1), 0)
                allowed = (key_seg == query_seg) & (key_pos <= query_pos)
                masks[tile, index, second * half : (second + 1) * half, :] = jnp.where(
                    allowed, 0.0, NEG_LARGE
                )
            return unused

        lax.fori_loop(first, end, fill, 0)


def split_heads(tile_rows, scale=None):
    half = tile_rows.shape[0]
    if scale is not None:
        tile_rows = tile_rows * jnp.asarray(scale, tile_rows.dtype)
    lane = lax.broadcasted_iota(jnp.int32, (half, 128), 1)
    zero = jnp.zeros((half, 128), tile_rows.dtype)
    t0, t1, t2 = (tile_rows[:, 128 * k : 128 * k + 128] for k in range(3))

    def low(t):
        return jnp.where(lane < 64, t, zero)

    def high(t):
        return jnp.where(lane >= 64, t, zero)

    straight = jnp.concatenate([low(t0), low(t1), high(t1), high(t2)], axis=0)
    crossed = jnp.concatenate([high(t0), low(t2)], axis=0)
    return straight, crossed


def join_heads(straight_t, crossed_t, half):
    def head(t, k, upper):
        return t[64 * upper : 64 * upper + 64, half * k : half * k + half]

    tiles = (
        (head(straight_t, 0, 0), head(crossed_t, 0, 1)),
        (head(straight_t, 1, 0), head(straight_t, 2, 1)),
        (head(crossed_t, 1, 0), head(straight_t, 3, 1)),
    )
    return jnp.concatenate([jnp.concatenate(t, axis=0).T for t in tiles], axis=1)


def cross(v):
    return jnp.concatenate([v[:, 64:], v[:, :64]], axis=1)


def attention_forward(q, keys, seg_col, seg_row, ids, nz):
    rows = q.shape[0]
    half = rows // 2
    slots = nz + 1
    count = len(keys)
    slot = 2 * half
    lanes = 6 * half

    def kernel(ids_ref, q_ref, col_ref, row_ref, *refs):
        key_refs = refs[:count]
        out_ref, lse_ref, kv, scores, masks, sems = refs[count:]
        copies = load_keys(nz, half, ids_ref, key_refs, kv, sems)
        fill_masks(nz, half, ids_ref, col_ref, row_ref, masks)
        for copy in copies:
            copy.wait()
        for tile in range(2):
            first, end = slot_range(nz, ids_ref, tile)
            for pair in range(PAIRS):
                straight, crossed = split_heads(
                    q_ref[tile * half : (tile + 1) * half, 384 * pair : 384 * pair + 384], SCALE
                )

                def score(index, peak):
                    at = pl.ds(pl.multiple_of(index * slot, slot), slot)
                    k = kv[at, 128 * pair : 128 * pair + 128]
                    mask = masks[tile, index]
                    s = jnp.concatenate([nt(k, straight), nt(cross(k), crossed)], axis=1)
                    s = s + jnp.concatenate([mask] * 6, axis=1)
                    scores[index] = s
                    return jnp.maximum(peak, jnp.max(s, axis=0, keepdims=True))

                peak = lax.fori_loop(
                    first, end, score, jnp.full((1, lanes), NEG_LARGE, F32)
                )

                def mix(index, carry):
                    mass, out_s, out_c = carry
                    at = pl.ds(pl.multiple_of(index * slot, slot), slot)
                    v = kv[at, 512 + 128 * pair : 512 + 128 * pair + 128]
                    p = jnp.exp(scores[index] - peak)
                    mass = mass + jnp.sum(p, axis=0, keepdims=True)
                    p = p.astype(BF)
                    v_t = v.T
                    out_s = out_s + nn(v_t, p[:, : 4 * half])
                    out_c = out_c + nn(
                        jnp.concatenate([v_t[64:], v_t[:64]], axis=0), p[:, 4 * half :]
                    )
                    return mass, out_s, out_c

                mass, out_s, out_c = lax.fori_loop(
                    first,
                    end,
                    mix,
                    (
                        jnp.zeros((1, lanes), F32),
                        jnp.zeros((128, 4 * half), F32),
                        jnp.zeros((128, 2 * half), F32),
                    ),
                )
                share = 1.0 / mass
                out_s = out_s * share[:, : 4 * half]
                out_c = out_c * share[:, 4 * half :]
                out_ref[tile * half : (tile + 1) * half, 384 * pair : 384 * pair + 384] = (
                    join_heads(out_s, out_c, half).astype(BF)
                )
                spot = tile * PAIRS + pair
                lse_ref[spot : spot + 1, :] = peak + jnp.log(mass)

    pairs = slots * slot * half * HEADS
    return pl.pallas_call(
        kernel,
        out_shape=(shape(q.shape, BF), shape((2 * PAIRS, lanes), F32)),
        in_specs=[SMEM, VMEM, VMEM, VMEM] + [ANY] * count,
        out_specs=(VMEM, VMEM),
        scratch_shapes=[
            pltpu.VMEM((slots * slot, 1024), BF),
            pltpu.VMEM((slots, slot, lanes), F32),
            pltpu.VMEM((2, slots, slot, half), F32),
            pltpu.SemaphoreType.DMA((2, nz + 1)),
        ],
        compiler_params=params(),
        cost_estimate=cost(8 * 256 * pairs, 2 * slots * slot * 1024, pairs),
        name="attend",
    )(ids, q, seg_col, seg_row, *keys)


def attention_backward(q, keys, seg_col, seg_row, attended, grad_att, lse, ids, nz, after=()):
    rows = q.shape[0]
    half = rows // 2
    slots = nz + 1
    count = len(keys)
    slot = 2 * half
    lanes = 6 * half

    def kernel(ids_ref, q_ref, col_ref, row_ref, att_ref, grad_ref, lse_ref, *refs):
        key_refs = refs[:count]
        dq_ref, mine_ref, other_ref, kv, dkv, masks, sems = refs[count + len(after) :]
        copies = load_keys(nz, half, ids_ref, key_refs, kv, sems)
        fill_masks(nz, half, ids_ref, col_ref, row_ref, masks)
        dkv[...] = jnp.zeros_like(dkv)
        for copy in copies:
            copy.wait()
        for tile in range(2):
            first, end = slot_range(nz, ids_ref, tile)
            for pair in range(PAIRS):
                here = (slice(tile * half, (tile + 1) * half), slice(384 * pair, 384 * pair + 384))
                q_s, q_c = split_heads(q_ref[here], SCALE)
                g_s, g_c = split_heads(grad_ref[here])
                product = grad_ref[here].astype(F32) * att_ref[here].astype(F32)
                turned = [product[:, 128 * k : 128 * k + 128].T for k in range(3)]
                lower = [jnp.sum(t[:64], axis=0, keepdims=True) for t in turned]
                upper = [jnp.sum(t[64:], axis=0, keepdims=True) for t in turned]
                delta = jnp.concatenate(
                    [lower[0], lower[1], upper[1], upper[2], upper[0], lower[2]], axis=1
                )
                spot = tile * PAIRS + pair
                total = lse_ref[spot : spot + 1, :]

                def step(index, carry):
                    dq_s, dq_c = carry
                    at = pl.ds(pl.multiple_of(index * slot, slot), slot)
                    k_lanes = slice(128 * pair, 128 * pair + 128)
                    v_lanes = slice(512 + 128 * pair, 512 + 128 * pair + 128)
                    k, v = kv[at, k_lanes], kv[at, v_lanes]
                    mask = masks[tile, index]
                    s = jnp.concatenate([nt(k, q_s), nt(cross(k), q_c)], axis=1)
                    p = jnp.exp(s + jnp.concatenate([mask] * 6, axis=1) - total)
                    dp = jnp.concatenate([nt(v, g_s), nt(cross(v), g_c)], axis=1)
                    ds = (p * (dp - delta)).astype(BF)
                    p = p.astype(BF)
                    dkv[at, v_lanes] += nn(p[:, : 4 * half], g_s) + cross(
                        nn(p[:, 4 * half :], g_c)
                    )
                    dkv[at, k_lanes] += nn(ds[:, : 4 * half], q_s) + cross(
                        nn(ds[:, 4 * half :], q_c)
                    )
                    k_t = k.T
                    dq_s = dq_s + nn(k_t, ds[:, : 4 * half])
                    dq_c = dq_c + nn(
                        jnp.concatenate([k_t[64:], k_t[:64]], axis=0), ds[:, 4 * half :]
                    )
                    return dq_s, dq_c

                dq_s, dq_c = lax.fori_loop(
                    first,
                    end,
                    step,
                    (jnp.zeros((128, 4 * half), F32), jnp.zeros((128, 2 * half), F32)),
                )
                dq_ref[here] = (SCALE * join_heads(dq_s, dq_c, half)).astype(BF)
        for index in range(slots):
            mine_ref[index] = dkv[index * slot : index * slot + half, :].astype(BF)
            other_ref[index] = dkv[index * slot + half : (index + 1) * slot, :].astype(BF)

    pairs = slots * slot * half * HEADS
    return pl.pallas_call(
        kernel,
        out_shape=(
            shape(q.shape, BF),
            shape((slots, half, 1024), BF),
            shape((slots, half, 1024), BF),
        ),
        in_specs=[SMEM] + [VMEM] * 6 + [ANY] * (count + len(after)),
        out_specs=(VMEM,) * 3,
        scratch_shapes=[
            pltpu.VMEM((slots * slot, 1024), BF),
            pltpu.VMEM((slots * slot, 1024), F32),
            pltpu.VMEM((2, slots, slot, half), F32),
            pltpu.SemaphoreType.DMA((2, nz + 1)),
        ],
        compiler_params=params(),
        cost_estimate=cost(300 * 256 * pairs, 2 * slots * slot * 1024, pairs),
        name="attend_back",
    )(ids, q, seg_col, seg_row, attended, grad_att, lse, *keys, *after)


def out_project(tokens, attended, gain, weight, ids, ny, shard):
    rows, width = tokens.shape
    count, moves = len(weight.arrays), len(weight.places)

    def kernel(ids_ref, tokens_ref, att_ref, gain_ref, *refs):
        pieces = refs[:count]
        resid_ref, norm_ref, held, sems = refs[count:]
        for copy in start_load(pieces, weight.places, held, sems, ids_ref, ny, shard, width // 2):
            copy.wait()
        resid = tokens_ref[...].astype(F32) + nn(att_ref[...], held[...])
        resid_ref[...] = resid
        norm_ref[...] = (resid * inv_root(resid) * gain_ref[...]).astype(BF)

    return pl.pallas_call(
        kernel,
        out_shape=(shape((rows, width), F32), shape((rows, width), BF)),
        in_specs=[SMEM] + [VMEM] * 3 + [ANY] * count,
        out_specs=(VMEM, VMEM),
        scratch_shapes=[pltpu.VMEM((width, width), BF), pltpu.SemaphoreType.DMA((moves,))],
        compiler_params=params(),
        cost_estimate=cost(2 * rows * width * width, 2 * width * width + 10 * rows * width),
        name="out_project",
    )(ids, tokens, attended, gain, *weight.arrays)


def out_back(resid, cotangent, gain, terms, weight, ids, ny, shard, after=()):
    rows, width = resid.shape
    count, moves = len(weight.arrays), len(weight.places)
    term_count = len(terms)

    def kernel(ids_ref, resid_ref, cot_ref, gain_ref, *refs):
        term_refs, pieces = refs[:term_count], refs[term_count : term_count + count]
        gres_ref, branch_ref, gatt_ref, ggain_ref, held, sems = refs[term_count + count + len(after) :]
        copies = start_load(pieces, weight.places, held, sems, ids_ref, ny, shard, width // 2)
        grad_norm = term_refs[0][...].astype(F32)
        for ref in term_refs[1:]:
            grad_norm = grad_norm + ref[...].astype(F32)
        resid = resid_ref[...]
        root = inv_root(resid)
        s = resid * root
        ggain_ref[...] = jnp.sum(grad_norm * s, axis=0, keepdims=True)
        t = grad_norm * gain_ref[...]
        gres = cot_ref[...].astype(F32) + root * (
            t - s * jnp.mean(t * s, axis=-1, keepdims=True)
        )
        gres_ref[...] = gres
        branch = gres.astype(BF)
        branch_ref[...] = branch
        for copy in copies:
            copy.wait()
        gatt_ref[...] = nt(branch, held[...]).astype(BF)

    return pl.pallas_call(
        kernel,
        out_shape=(
            shape((rows, width), F32),
            shape((rows, width), BF),
            shape((rows, width), BF),
            shape((1, width), F32),
        ),
        in_specs=[SMEM] + [VMEM] * (3 + term_count) + [ANY] * (count + len(after)),
        out_specs=(VMEM,) * 4,
        scratch_shapes=[pltpu.VMEM((width, width), BF), pltpu.SemaphoreType.DMA((moves,))],
        compiler_params=params(),
        cost_estimate=cost(2 * rows * width * width, 2 * width * width + 20 * rows * width),
        name="out_back",
    )(ids, resid, cotangent, gain, *terms, *weight.arrays, *after)


def in_back(tokens, gres, gain, dq, dkv, weight_q, weight_kv, ids, ny, shard, after=()):
    rows, width = tokens.shape
    kv_width = dkv.shape[1]
    count_q, count_kv = len(weight_q.arrays), len(weight_kv.arrays)

    def kernel(ids_ref, tokens_ref, gres_ref, gain_ref, dq_ref, dkv_ref, *refs):
        q_pieces, kv_pieces = refs[:count_q], refs[count_q : count_q + count_kv]
        out_ref, ggain_ref, held_q, held_kv, sems_q, sems_kv = refs[count_q + count_kv + len(after) :]
        copies = start_load(
            kv_pieces, weight_kv.places, held_kv, sems_kv, ids_ref, ny, shard, kv_width // 2
        ) + start_load(q_pieces, weight_q.places, held_q, sems_q, ids_ref, ny, shard, width // 2)
        for copy in copies:
            copy.wait()
        grad_norm = nt(dq_ref[...], held_q[...]) + nt(dkv_ref[...], held_kv[...])
        x = tokens_ref[...].astype(F32)
        root = inv_root(x)
        s = x * root
        ggain_ref[...] = jnp.sum(grad_norm * s, axis=0, keepdims=True)
        t = grad_norm * gain_ref[...]
        out_ref[...] = gres_ref[...] + root * (t - s * jnp.mean(t * s, axis=-1, keepdims=True))

    return pl.pallas_call(
        kernel,
        out_shape=(shape((rows, width), F32), shape((1, width), F32)),
        in_specs=[SMEM] + [VMEM] * 5 + [ANY] * (count_q + count_kv + len(after)),
        out_specs=(VMEM, VMEM),
        scratch_shapes=[
            pltpu.VMEM((width, width), BF),
            pltpu.VMEM((width, kv_width), BF),
            pltpu.SemaphoreType.DMA((len(weight_q.places),)),
            pltpu.SemaphoreType.DMA((len(weight_kv.places),)),
        ],
        compiler_params=params(),
        cost_estimate=cost(
            2 * rows * width * (width + kv_width), 2 * width * (width + kv_width) + 12 * rows * width
        ),
        name="in_back",
    )(ids, tokens, gres, gain, dq, dkv, *weight_q.arrays, *weight_kv.arrays, *after)


def expert_block(block_ids, blocks, cot_all, coeffs, w_gate, w_up, w_down, out_dtype, after=()):
    experts, width, units = w_gate.shape
    pieces = [p for block in blocks for p in block]
    count, many, extra = len(pieces), len(blocks), len(after)
    size = coeffs[0].shape[0]
    rows = many * size

    def kernel(id_ref, *refs):
        n_refs, refs = refs[:count], refs[count:]
        c_refs, refs = refs[:many], refs[many:]
        (coeff_ref, wg_ref, wu_ref, wd_ref), refs = refs[:4], refs[4 + extra :]
        (hid_ref, gg_ref, gu_ref), refs = refs[:3], refs[3:]
        mix_refs, gnf_refs, (mix, gnf) = refs[:many], refs[many : 2 * many], refs[2 * many :]
        e = pl.program_id(0)
        wg, wu, wd = wg_ref[0], wu_ref[0], wd_ref[0]
        rows_in = jnp.concatenate([ref[...] for ref in n_refs], axis=0)
        cot = jnp.concatenate([ref[...] for ref in c_refs], axis=0)
        lane = lax.broadcasted_iota(jnp.int32, coeff_ref.shape, 1)
        weight = jnp.sum(jnp.where(lane == e, coeff_ref[...], 0.0), axis=1, keepdims=True)
        gate = nn(rows_in, wg)
        up = nn(rows_in, wu)
        back = nt(cot, wd) * weight
        sigma = jax.nn.sigmoid(gate)
        silu = gate * sigma
        hidden = (silu * up * weight).astype(BF)
        grad_gate = (back * up * sigma * (1.0 + gate * (1.0 - sigma))).astype(BF)
        grad_up = (back * silu).astype(BF)
        hid_ref[...] = hidden
        gg_ref[...] = grad_gate
        gu_ref[...] = grad_up
        more = nt(grad_gate, wg) + nt(grad_up, wu)
        out = nn(hidden, wd)

        @pl.when(e == 0)
        def _():
            gnf[...] = more
            mix[...] = out

        @pl.when(e > 0)
        def _():
            gnf[...] += more
            mix[...] += out

        @pl.when(e == experts - 1)
        def _():
            for k in range(many):
                here = slice(k * size, (k + 1) * size)
                gnf_refs[k][...] = gnf[here].astype(out_dtype)
                mix_refs[k][...] = mix[here].astype(out_dtype)

    keep = pl.BlockSpec((size, width), lambda e, s: (0, 0))
    unit = pl.BlockSpec((rows, units), lambda e, s: (0, e))
    outs = pl.pallas_call(
        kernel,
        grid_spec=pltpu.PrefetchScalarGridSpec(
            num_scalar_prefetch=1,
            grid=(experts,),
            in_specs=[pl.BlockSpec(p.shape, lambda e, s: (0, 0)) for p in pieces]
            + [pl.BlockSpec((size, width), lambda e, s, k=k: (s[k], 0)) for k in range(many)]
            + [
                pl.BlockSpec((rows, experts), lambda e, s: (0, 0)),
                pl.BlockSpec((1, width, units), lambda e, s: (e, 0, 0)),
                pl.BlockSpec((1, width, units), lambda e, s: (e, 0, 0)),
                pl.BlockSpec((1, units, width), lambda e, s: (e, 0, 0)),
            ]
            + [ANY] * extra,
            out_specs=(unit,) * 3 + (keep,) * (2 * many),
            scratch_shapes=[pltpu.VMEM((rows, width), F32)] * 2,
        ),
        out_shape=(shape((rows, experts * units), BF),) * 3
        + (shape((size, width), out_dtype),) * (2 * many),
        compiler_params=params(),
        cost_estimate=cost(
            12 * rows * width * experts * units, 6 * experts * width * units + 10 * rows * width
        ),
        name="experts",
    )(
        block_ids,
        *pieces,
        *[cot_all] * many,
        jnp.concatenate(coeffs, axis=0),
        w_gate,
        w_up,
        w_down,
        *after,
    )
    return outs[:3], outs[3 : 3 + many], outs[3 + many :]


def expert_grads(block_ids, pieces, cot_all, hidden, grad_gate, grad_up, experts, size):
    groups = len(hidden)
    width = cot_all.shape[1]
    units = hidden[0].shape[1] // experts
    count = len(pieces)
    blocks = block_ids.shape[0]
    rows = blocks * size

    def kernel(id_ref, *refs):
        n_refs, c_ref = refs[:count], refs[count]
        at = count + 1
        h_refs, gg_refs, gu_refs = (
            refs[at : at + groups],
            refs[at + groups : at + 2 * groups],
            refs[at + 2 * groups : at + 3 * groups],
        )
        out_ref, n_all, c_all, n_sems, c_sems = refs[at + 3 * groups :]

        @pl.when(pl.program_id(0) == 0)
        def _():
            copies, row = [], 0
            for k, ref in enumerate(n_refs):
                copies.append(
                    pltpu.make_async_copy(ref, n_all.at[pl.ds(row, ref.shape[0])], n_sems.at[k])
                )
                row += ref.shape[0]
            for k in range(blocks):
                start = pl.multiple_of(id_ref[k] * size, size)
                copies.append(
                    pltpu.make_async_copy(
                        c_ref.at[pl.ds(start, size)], c_all.at[pl.ds(k * size, size)], c_sems.at[k]
                    )
                )
            for copy in copies:
                copy.start()
            for copy in copies:
                copy.wait()

        grads = jnp.concatenate(
            [
                jnp.concatenate([ref[...] for ref in gg_refs], axis=0),
                jnp.concatenate([ref[...] for ref in gu_refs], axis=0),
            ],
            axis=1,
        )
        out_ref[:, : 2 * units] = tn(n_all[...], grads).astype(BF)
        hid = jnp.concatenate([ref[...] for ref in h_refs], axis=0)
        out_ref[:, 2 * units :] = tn(c_all[...], hid).astype(BF)

    grid_spec = pltpu.PrefetchScalarGridSpec(
        num_scalar_prefetch=1,
        grid=(experts,),
        in_specs=[ANY] * (count + 1)
        + [
            pl.BlockSpec((one.shape[0], units), lambda e, s: (0, e))
            for group in (hidden, grad_gate, grad_up)
            for one in group
        ],
        out_specs=pl.BlockSpec((width, 3 * units), lambda e, s: (e, 0)),
        scratch_shapes=[
            pltpu.VMEM((rows, width), BF),
            pltpu.VMEM((rows, width), BF),
            pltpu.SemaphoreType.DMA((count,)),
            pltpu.SemaphoreType.DMA((blocks,)),
        ],
    )
    return pl.pallas_call(
        kernel,
        grid_spec=grid_spec,
        out_shape=shape((experts * width, 3 * units), BF),
        compiler_params=params(),
        cost_estimate=cost(
            6 * rows * width * units * experts, 4 * rows * width + 6 * experts * units * width
        ),
        name="expert_grads",
    )(block_ids, *pieces, cot_all, *hidden, *grad_gate, *grad_up)


def spread_grads(grads, experts):
    width, units = grads.shape[0] // experts, grads.shape[1] // 3

    def kernel(in_ref, gate_ref, up_ref, down_ref):
        gate_ref[0] = in_ref[:, :units].astype(F32)
        up_ref[0] = in_ref[:, units : 2 * units].astype(F32)
        down_ref[0] = in_ref[:, 2 * units :].astype(F32).T

    side = pl.BlockSpec((1, width, units), lambda e: (e, 0, 0))
    return pl.pallas_call(
        kernel,
        grid=(experts,),
        out_shape=(shape((experts, width, units), F32),) * 2
        + (shape((experts, units, width), F32),),
        in_specs=[pl.BlockSpec((width, 3 * units), lambda e: (e, 0))],
        out_specs=(side, side, pl.BlockSpec((1, units, width), lambda e: (e, 0, 0))),
        compiler_params=params(),
        cost_estimate=cost(0, 6 * grads.size),
        name="spread_grads",
    )(grads)


def tie(values, *after):
    return pl.pallas_call(
        lambda *refs: None,
        out_shape=[shape(v.shape, v.dtype) for v in values],
        in_specs=[ANY] * (len(values) + len(after)),
        out_specs=[ANY] * len(values),
        input_output_aliases={k: k for k in range(len(values))},
        compiler_params=params(),
        cost_estimate=cost(0, 0),
        name="tie",
    )(*values, *after)


def weight_grads(ids, pairs, extra=(), after=()):
    depth = pairs[0][0].shape[1]
    halves = [right.shape[1] // 2 for _, right in pairs]
    width = sum(halves) + (128 if extra else 0)
    rows = pairs[0][0].shape[0]
    inputs = 2 * len(pairs) + len(extra)

    def kernel(ids_ref, *refs):
        mine_ref, other_ref = refs[inputs + len(after) :]
        core, at = ids_ref[1], 0
        for k, n in enumerate(halves):
            left, right = refs[2 * k][...], refs[2 * k + 1]
            for out_ref, side in ((mine_ref, core), (other_ref, 1 - core)):
                columns = right[:, pl.ds(pl.multiple_of(side * n, 128), n)]
                out_ref[:, at : at + n] = tn(left, columns).astype(BF)
            at += n
        if extra:
            lines = [ref[...] for ref in refs[2 * len(pairs) : inputs]]
            lines.append(jnp.zeros((128 - len(extra), depth), F32))
            turned = jnp.concatenate(lines, axis=0).T.astype(BF)
            mine_ref[:, at:] = turned
            other_ref[:, at:] = turned

    return pl.pallas_call(
        kernel,
        out_shape=(shape((depth, width), BF),) * 2,
        in_specs=[SMEM] + [VMEM] * inputs + [ANY] * len(after),
        out_specs=(VMEM,) * 2,
        compiler_params=params(),
        cost_estimate=cost(4 * rows * depth * width, 4 * depth * width),
        name="weight_grads",
    )(ids, *[v for pair in pairs for v in pair], *extra, *after)


def body(
    tokens,
    segments,
    routes,
    route_weights,
    gain_attn,
    w_query,
    w_key,
    w_value,
    w_out,
    gain_ffn,
    w_gate,
    w_up,
    w_down,
    cotangent,
):
    tokens, cotangent = tokens[0], cotangent[0]
    rows, width = tokens.shape
    half = rows // 2
    nz, ny = lax.axis_size("z"), lax.axis_size("y")
    z, core, y, x = (lax.axis_index(a) for a in ("z", "core", "y", "x"))
    ids = jnp.stack([z, core, y, x]).astype(jnp.int32)
    shard = w_query.shape[0]
    experts = w_gate.shape[0]
    kv_width = w_key.shape[1] + w_value.shape[1]
    plane = [(dy, dx) for dy in range(ny) for dx in range(2)]
    seg_row = segments
    seg_col = segments.reshape(-1, 1)

    chosen = routes[0][:, :, None] == jnp.arange(experts, dtype=jnp.int32)[None, None, :]
    coeff = jnp.sum(jnp.where(chosen, route_weights[0][:, :, None], 0.0), axis=1)
    small = jnp.concatenate(
        [coeff.reshape(-1), gain_attn.astype(F32), gain_ffn.astype(F32)]
    ).reshape(-1, 128)
    coeffs = {}
    slot = jnp.arange(2 * ny, dtype=jnp.int32)[None, :, None]
    gains = jnp.zeros((2, 2 * ny, shard), F32)
    owners = {}
    for dy, dx in plane:
        got = small if (dy, dx) == (0, 0) else to_plane(small, -dy % ny, dx)
        got = got.reshape(-1)
        owner = lax.rem(y + dy, ny) * 2 + (x if dx == 0 else 1 - x)
        owners[(dy, dx)] = owner.astype(jnp.int32).reshape(1)
        coeffs[(dy, dx)] = got[: rows * experts].reshape(rows, experts)
        pair = got[rows * experts :].reshape(2, 1, shard)
        gains = gains + jnp.where(slot == owner, pair, 0.0)
    gain_a, gain_f = gains[0].reshape(1, width), gains[1].reshape(1, width)

    weight_kv = gather_first(w_key, w_value, core)
    weight_q, weight_o = gather_rest(w_query, w_out, core)
    cot_all = lax.all_gather(cotangent, ("y", "x"), axis=0, tiled=True)

    x_f = tokens.astype(F32)
    normed = (x_f * inv_root(x_f) * gain_a).astype(BF)
    kv = gathered_matmul(normed, weight_kv, ids, ny, shard, kv_width)
    beside = swap(kv, "core")
    came = []
    for d in range(1, nz):
        start = jnp.where(z + d < nz, 0, half)
        piece = lax.dynamic_slice_in_dim(kv, start, half, 0)
        came.append(lax.ppermute(piece, "z", [(i, (i + d) % nz) for i in range(nz)]))
    came = jnp.stack(came)
    keys = [kv, beside, came, swap(came, "core")]
    queries = gathered_matmul(normed, weight_q, ids, ny, shard, width)
    attended, lse = attention_forward(queries, keys, seg_col, seg_row, ids, nz)
    resid, normed_f = out_project(tokens, attended, gain_f, weight_o, ids, ny, shard)

    from_x = swap(normed_f, "x")
    norms = {(0, 0): [normed_f], (0, 1): [from_x]}
    for d in range(1, ny):
        side = from_y(normed_f, d)
        norms[(d, 0)] = [side]
        norms[(d, 1)] = [from_y(from_x[:half], d), swap(side[half:], "x")]
    groups = [
        [(0, 0)],
        [(0, 1)] + [(d, 0) for d in range(1, ny)],
        [(d, 1) for d in range(1, ny)],
    ]
    hidden, grad_gate, grad_up, mixes, grad_norms, after = [], [], [], [], [], ()
    for group in groups:
        own = group == [(0, 0)]
        (h, gg, gu), mix, gnf = expert_block(
            jnp.concatenate([jnp.zeros_like(owners[where]) if own else owners[where] for where in group]),
            [norms[where] for where in group],
            cotangent if own else cot_all,
            [coeffs[where] for where in group],
            w_gate,
            w_up,
            w_down,
            F32 if own else BF,
            after,
        )
        after = (h,)
        hidden.append(h)
        grad_gate.append(gg)
        grad_up.append(gu)
        for where, one, two in zip(group, mix, gnf):
            mixes.append(one)
            grad_norms.append(two if own else to_plane(two, *where))
    order = [where for group in groups for where in group]
    expert_parts = expert_grads(
        jnp.concatenate([owners[where] for where in order]),
        [piece for where in order for piece in norms[where]],
        cot_all,
        hidden,
        grad_gate,
        grad_up,
        experts,
        rows,
    )
    expert_shard = lax.psum_scatter(
        expert_parts, ("z", "core"), scatter_dimension=0, tiled=True
    )
    gres, branch, grad_att, ggain_f = out_back(
        resid, cotangent, gain_f, grad_norms, weight_o, ids, ny, shard, (expert_parts,)
    )
    mixes[1:] = tie(mixes[1:], branch)
    result, came = resid, []
    for where, mix in zip(order, mixes):
        mix = mix if where == (0, 0) else to_plane(mix, *where)
        came.append(mix)
        result = result + mix.astype(F32)
    result = result.astype(BF)
    o_grads = weight_grads(ids, [(attended, branch)])
    dq, dkv_mine, dkv_other = attention_backward(
        queries, keys, seg_col, seg_row, attended, grad_att, lse, ids, nz, o_grads[:1]
    )
    q_grads = weight_grads(ids, [(normed, dq)], (), came[1:])
    parts = add_low(dkv_mine, swap(dkv_other, "core"))
    low = parts[0].astype(F32)
    high = lax.dynamic_index_in_dim(parts, z + 1, 0, keepdims=False).astype(F32)
    for d in range(1, nz):
        index = jnp.where(d <= z, d, z + 1 + nz - d)
        piece = lax.dynamic_index_in_dim(parts, index, 0, keepdims=False)
        got = lax.ppermute(piece, "z", [((i + d) % nz, i) for i in range(nz)]).astype(F32)
        low = low + jnp.where(z + d < nz, got, 0.0)
        high = high + jnp.where(z + d < nz, 0.0, got)
    dkv = jnp.concatenate([low, high], axis=0).astype(BF)
    o_blocks, q_blocks = plane_blocks(*o_grads, y, x), plane_blocks(*q_grads, y, x)
    o_total, q_total = plane_total(o_blocks), plane_total(q_blocks)
    grad_tokens, ggain_a = in_back(
        tokens, gres, gain_a, dq, dkv, weight_q, weight_kv, ids, ny, shard
    )
    (expert_shard,) = tie([expert_shard], o_total, grad_tokens)
    expert_totals = spread_grads(
        lax.all_gather(expert_shard, ("z", "core"), axis=0, tiled=True), experts
    )
    kv_grads = weight_grads(ids, [(normed, dkv)], (ggain_a, ggain_f))
    kv_blocks = plane_blocks(*kv_grads, y, x)
    o_total, q_total = tie([o_total, q_total], *kv_blocks.values())
    o_first, q_first = z_first(o_total), z_first(q_total)
    kv_first = z_first(plane_total(kv_blocks))
    grad_wo = jnp.concatenate(whole_grad(z_rest(o_first, z), core), axis=1)
    grad_wq = jnp.concatenate(whole_grad(z_rest(q_first, z), core), axis=1)
    grad_wk, grad_wv = whole_grad(z_rest(kv_first, z), core)
    ggain_a, ggain_f = grad_wk[:, -128], grad_wk[:, -127]
    grad_wk, grad_wv = grad_wk[:, :-128], grad_wv[:, :-128]
    return (
        result[None],
        grad_tokens[None],
        ggain_a,
        grad_wq,
        grad_wk,
        grad_wv,
        grad_wo,
        ggain_f,
        *expert_totals,
    )


def solution(mesh):
    ctx, wt = mesh.shape["ctx"], mesh.shape["wt"]
    fine = Mesh(mesh.devices.reshape(ctx // 2, 2, wt // 2, 2), ("z", "core", "y", "x"))
    c, w = ("z", "core"), ("y", "x")
    rows = P(w, c, None)
    return jax.shard_map(
        body,
        mesh=fine,
        in_specs=(
            rows,
            P(w, None),
            rows,
            rows,
            P(w),
            P(w, None),
            P(w, None),
            P(w, None),
            P(w, None),
            P(w),
            P(None, None, w),
            P(None, None, w),
            P(None, w, None),
            rows,
        ),
        out_specs=(
            rows,
            rows,
            P(w),
            P(w, None),
            P(w, None),
            P(w, None),
            P(w, None),
            P(w),
            P(None, None, w),
            P(None, None, w),
            P(None, w, None),
        ),
        check_vma=False,
    )
```
